32 devices in a mesh: cfg: 2 (over core), req: 4 (over y, x), tp: 4 (over z).
Axes of the slice: x: 2, y: 2, z: 4, core: 2. Of those that a mesh axis runs over, the one named last changes fastest.
Arguments:
- latent: float32 [1536, 64], P(('req', 'tp')), may hold values from -6 to 6
- states: float32 [2, 1536, 1536], P('cfg', ('req', 'tp')), may hold values from -12 to 12
- token_counts: int32 [3], replicated, may hold values from 1 to 960, 1536 in all
- text_lens: int32 [2, 3], P('cfg'), may hold values from 1 to 512, 768 in all within a row
- steps_index: int32 [3], replicated, may hold values from 0 to 49
- modulation: float32 [3, 6, 1536], replicated, may hold values from -3 to 3
- self_qkv: bfloat16 [1536, 3, 1536], P(None, None, 'tp'), may hold values from -0.15625 to 0.15625
- self_out: bfloat16 [1536, 1536], P('tp'), may hold values from -0.15625 to 0.15625
- qk_gains: float32 [4, 1536], P(None, 'tp'), may hold values from 0.8 to 2
- cross_query: bfloat16 [1536, 1536], P(None, 'tp'), may hold values from -1 to 1
- cross_out: bfloat16 [1536, 1536], P('tp'), may hold values from -0.15625 to 0.15625
- cross_gain: float32 [1536], replicated, may hold values from 0.25 to 1.75
- text_kv: bfloat16 [2, 3, 2, 512, 1536], P('cfg', None, None, None, 'tp'), may hold values from -6 to 6
- ffn_in_weight: bfloat16 [8960, 1536], P(('cfg', 'tp')), may hold values from -0.15625 to 0.15625
- ffn_out_weight: bfloat16 [8960, 1536], P(('cfg', 'tp')), may hold values from -0.0625 to 0.0625
- head_weight: bfloat16 [1536, 64], replicated, may hold values from -0.15625 to 0.15625
Outputs:
- new_latent: float32 [1536, 64], P(('req', 'tp'), 'cfg')
- velocity: float32 [1536, 64], P(('req', 'tp'), 'cfg')
- peak: float32 [3], replicated
The draws below stay inside these ranges and needn't reach their ends.
Inputs may be any that keep to these rules, and one draw needn't show every extreme that they name: `token_counts`: the counts sum to 1536 and the largest is exactly 960. `text_lens`: in each prompt half the counts sum to 768 and the largest is exactly 512.
All inputs are finite; a program needn't handle non-finite values.
Results may differ from the reference program's by a relative error of at most 0.03.
Values may be sent and summed in bfloat16 or wider, within the bound.
A program may use at most 64 MiB of HBM per device.

```python
import math
import jax
import jax.numpy as jnp
import numpy as np
from jax import lax

D = 1536
HEADS = 12
HD = 128
FF = 8960
OUT = 64
TEXT = 512
REQS = 3
STEPS = 50
TOK_DEV = 384
HP = 12
TOKENS = 1536
MOST = 960
N_CFG = 2
N_TP = 4


def draw_cross_query(key, part):
    width = HP * HD
    base = jax.random.normal(jax.random.fold_in(key, 11), (D, width), jnp.float32)
    base = jnp.clip(base, -5.0, 5.0)
    head_pos = (jnp.arange(width, dtype=jnp.int32) // HD).astype(jnp.float32)
    ratio = jnp.minimum(head_pos / (HEADS - 1.0), 1.0)
    column_scale = jnp.exp(-ratio * jnp.log(3.0))
    values = base * column_scale[None, :] * D ** (-0.5)
    return values.astype(jnp.bfloat16)


def draw_states(key, part):
    frac = jnp.arange(TOKENS, dtype=jnp.int32).astype(jnp.float32) / (TOKENS - 1.0)
    base = jnp.clip(jax.random.normal(jax.random.fold_in(key, 23), (TOKENS, D), jnp.float32), -5.0, 5.0)
    fresh = jnp.clip(jax.random.normal(jax.random.fold_in(key, 24), (TOKENS, D), jnp.float32), -5.0, 5.0)
    weight_rise = 0.05 * jnp.exp(frac * jnp.log(30.0))
    second = jnp.clip(base + weight_rise[:, None] * fresh, -12.0, 12.0)
    return jnp.stack([base, second]).astype(jnp.float32)


def block_levels(own_key, shape, pieces, smallest, top_value):
    def one(dim, blocks):
        steps = jax.random.uniform(jax.random.fold_in(jax.random.fold_in(own_key, 6), dim), (blocks,), jnp.float32, smallest / len(pieces), top_value / len(pieces))
        return jnp.repeat(jnp.exp(steps), shape[dim] // blocks).reshape((-1,) + (1,) * (len(shape) - dim - 1))

    level = one(*pieces[0])
    for cut in pieces[1:]:
        level = level * one(*cut)
    return level


def length_profile(count, total, most, lean):
    weights = [(1 << 20) // math.isqrt(standing ** lean) + 1 for standing in range(2, count + 1)]
    rest, holding = total - most - (count - 1), [1] * (count - 1)
    while rest > 0:
        free = [i for i in range(count - 1) if holding[i] < most]
        whole, budget = sum([weights[i] for i in free]), rest
        for i in free:
            extra = min(most - holding[i], max(1, budget * weights[i] // whole), rest)
            holding[i] = holding[i] + extra
            rest = rest - extra
    return np.array([most] + holding)


def uneven(rng, number_of, total, limit, skew):
    if number_of == 2:
        one = jax.random.randint(rng, (), max(1, total - limit), min(limit, total - 1) + 1)
        return jnp.stack([one, total - one])
    sizes = jnp.asarray(length_profile(number_of, total, limit, skew), jnp.int32)
    couples = (number_of - 1) // 2
    donor, taker = sizes[1:1 + 2 * couples:2], sizes[2:2 + 2 * couples:2]
    slack = jnp.minimum(donor - 1, limit - taker)
    shifted = jax.random.randint(jax.random.fold_in(rng, 1), (couples,), 0, 1 << 20) % (slack + 1)
    sizes = sizes.at[1:1 + 2 * couples:2].set(donor - shifted).at[2:2 + 2 * couples:2].set(taker + shifted)
    return sizes[jax.random.permutation(jax.random.fold_in(rng, 2), number_of)]


def normal_values(key, dims, scale, bound, shards=(), held_as=jnp.bfloat16):
    entries = jax.random.normal(key, dims, jnp.float32) * scale
    if len(shards) > 0:
        entries = block_levels(key, dims, shards, -0.22, 0.18) * entries
    return jnp.clip(entries, min=-bound, max=bound).astype(held_as)


def setup_inputs(seed: int = 0) -> dict:
    keys = jax.random.split(jax.random.key(seed), 17)
    return {
        "latent": normal_values(keys[0], (TOKENS, OUT), 1.0, 6.0, ((0, 16),), jnp.float32),
        "states": draw_states(jax.random.fold_in(keys[16], 71), 0),
        "token_counts": uneven(keys[2], REQS, TOKENS, MOST, 1).astype(jnp.int32),
        "text_lens": jax.vmap(lambda own: uneven(own, REQS, TEXT + TEXT // 2, TEXT, 1))(jax.random.split(keys[3], 2)).reshape((2, REQS)).astype(jnp.int32),
        "steps_index": jax.random.randint(keys[4], (REQS,), 0, STEPS).astype(jnp.int32),
        "modulation": normal_values(keys[5], (REQS, 6, D), 0.5, 3.0, (), jnp.float32),
        "self_qkv": normal_values(keys[6], (D, 3, HP * HD), D ** -0.5, 0.15625, ((2, 4),)),
        "self_out": normal_values(keys[7], (HP * HD, D), D ** -0.5, 0.15625, ((0, 4),)),
        "qk_gains": jnp.clip(jnp.exp(math.log(2.0) - 0.9162907 * jax.random.uniform(keys[8], (4, HP * HD), jnp.float32) ** block_levels(keys[8], (4, HP * HD), ((1, 4),), -0.2, 0.2)), 0.8, 2.0),
        "cross_query": draw_cross_query(jax.random.fold_in(keys[16], 71), 0),
        "cross_out": normal_values(keys[10], (HP * HD, D), D ** -0.5, 0.15625, ((0, 4),)),
        "cross_gain": jnp.clip(1.0 + 0.15 * jax.random.normal(keys[11], (D,), jnp.float32), 0.25, 1.75),
        "text_kv": normal_values(keys[12], (2, REQS, 2, TEXT, HP * HD), 1.0, 6.0, ((0, 2), (4, 4))),
        "ffn_in_weight": normal_values(keys[13], (FF, D), D ** -0.5, 0.15625, ((0, 8),)),
        "ffn_out_weight": normal_values(keys[14], (FF, D), FF ** -0.5, 0.0625, ((0, 8),)),
        "head_weight": normal_values(keys[15], (D, OUT), D ** -0.5, 0.15625),
    }


guide_scale = 5.0
rescale_mix = 0.7
flow_shift = 5.0
norm_eps = 1e-06
stat_eps = 1e-05

def layer_norm(values):
    average = lax.optimization_barrier(jnp.mean(values, axis=-1, keepdims=True))
    centered = values - average
    spread = lax.optimization_barrier(jnp.mean(centered * centered, axis=-1, keepdims=True))
    return centered * lax.rsqrt(spread + norm_eps)

def rms_norm(values, gains):
    real = values[:, :D]
    power = lax.optimization_barrier(jnp.mean(real * real, axis=1, keepdims=True))
    return (real * lax.rsqrt(power + norm_eps) * gains[:D]).astype(jnp.bfloat16)

def request_of(positions, request_ends):
    return lax.optimization_barrier(jnp.sum((positions[:, None] >= request_ends[None, :]).astype(jnp.int32), axis=1))

def presence(request_ids, request_count):
    return jnp.any(request_ids[:, None] == jnp.arange(request_count, dtype=jnp.int32)[None, :], axis=0)

def attend(running, queries, query_req, key_rows, value_rows, key_req, head_count, head_width):
    numerator, denominator = running
    query_count = queries.shape[0]
    key_count = key_rows.shape[0]
    query_wide = queries.astype(jnp.float32).reshape(query_count, head_count, head_width)
    key_wide = key_rows.astype(jnp.float32).reshape(key_count, head_count, head_width)
    scores = jnp.einsum('qhd,khd->hqk', query_wide, key_wide) * head_width ** (-0.5)
    same_req = query_req[:, None] == key_req[None, :]
    weights = jnp.where(same_req[None, :, :], jnp.exp(scores), 0.0)
    rounded = lax.optimization_barrier(weights.astype(jnp.bfloat16)).astype(jnp.float32)
    value_wide = value_rows.astype(jnp.float32).reshape(key_count, head_count, head_width)
    partial_sum = jnp.einsum('hqk,khd->qhd', rounded, value_wide)
    return (numerator + partial_sum.reshape(query_count, head_count * head_width), denominator + jnp.transpose(lax.optimization_barrier(jnp.sum(weights, axis=2))))

def finish_heads(running, head_count, head_width):
    numerator, denominator = running
    query_count = numerator.shape[0]
    mixed = numerator.reshape(query_count, head_count, head_width) / denominator[:, :, None]
    return mixed.reshape(query_count, head_count * head_width).astype(jnp.bfloat16)

def empty_state():
    return (jnp.zeros((TOK_DEV, D), jnp.float32), jnp.zeros((TOK_DEV, HEADS), jnp.float32))

def self_attention(queries, key_rows, value_rows, request_ids):
    blocks = TOKENS // TOK_DEV
    query_blocks = queries.reshape(blocks, TOK_DEV, D)
    key_blocks = key_rows.reshape(blocks, TOK_DEV, D)
    value_blocks = value_rows.reshape(blocks, TOK_DEV, D)
    request_blocks = request_ids.reshape(blocks, TOK_DEV)

    def per_block(inputs_pair):
        query_block, query_req = inputs_pair
        wanted = presence(query_req, REQS)

        def visit(running, key_inputs):
            key_block, value_block, key_req = key_inputs
            intersection = jnp.any(wanted & presence(key_req, REQS))

            def compute(current):
                return attend(current, query_block, query_req, key_block, value_block, key_req, HEADS, HD)

            def skip(current):
                return current
            return (lax.cond(intersection, compute, skip, running), None)
        final_state, unused = lax.scan(visit, empty_state(), (key_blocks, value_blocks, request_blocks))
        return finish_heads(final_state, HEADS, HD)
    return lax.map(per_block, (query_blocks, request_blocks)).reshape(TOKENS, D)

def cross_attention(queries, request_ids, text_half, lens_half, gains):
    blocks = TOKENS // TOK_DEV
    text_keys = rms_norm(text_half[:, 0].reshape(REQS * TEXT, HP * HD).astype(jnp.float32), gains)
    text_values = text_half[:, 1].reshape(REQS * TEXT, HP * HD)[:, :D]
    text_req = jnp.repeat(jnp.arange(REQS, dtype=jnp.int32), TEXT)
    text_pos = jnp.tile(jnp.arange(TEXT, dtype=jnp.int32), REQS)
    text_req = jnp.where(text_pos < lens_half[text_req], text_req, -1)

    def per_block(inputs_pair):
        query_block, query_req = inputs_pair
        final_state = attend(empty_state(), query_block, query_req, text_keys, text_values, text_req, HEADS, HD)
        return finish_heads(final_state, HEADS, HD)
    return lax.map(per_block, (queries.reshape(blocks, TOK_DEV, D), request_ids.reshape(blocks, TOK_DEV))).reshape(TOKENS, D)

def pad_heads(mixed):
    filler = jnp.zeros((mixed.shape[0], HP * HD - D), jnp.bfloat16)
    return jnp.concatenate([mixed, filler], axis=1)

def grouped_project(mixed, weight):
    group_cols = HP // N_TP * HD
    summed = jnp.zeros((mixed.shape[0], D), jnp.float32)
    for group_index in range(N_TP):
        lower = group_index * group_cols
        upper = lower + group_cols
        term = jnp.dot(mixed[:, lower:upper], weight[lower:upper], preferred_element_type=jnp.float32)
        summed = summed + lax.optimization_barrier(term.astype(jnp.bfloat16)).astype(jnp.float32)
    return summed

def feed_forward(rows, in_weight, out_weight):
    group_count = N_CFG * N_TP
    group_units = FF // group_count
    summed = jnp.zeros((rows.shape[0], D), jnp.float32)
    for group_index in range(group_count):
        lower = group_index * group_units
        upper = lower + group_units
        up_part = lax.dot_general(rows, in_weight[lower:upper], (((1,), (1,)), ((), ())), preferred_element_type=jnp.float32)
        activated = jax.nn.gelu(up_part, approximate=True).astype(jnp.bfloat16)
        term = jnp.dot(activated, out_weight[lower:upper], preferred_element_type=jnp.float32)
        summed = summed + lax.optimization_barrier(term.astype(jnp.bfloat16)).astype(jnp.float32)
    return summed

def request_mod(modulation, request_ids, which):
    return modulation[:, which][request_ids]

def noise_level(step_value):
    fraction = 1.0 - step_value / STEPS
    return flow_shift * fraction / (1.0 + (flow_shift - 1.0) * fraction)

def reference(latent, states, token_counts, text_lens, steps_index, modulation, self_qkv, self_out, qk_gains, cross_query, cross_out, cross_gain, text_kv, ffn_in_weight, ffn_out_weight, head_weight):
    request_ends = jnp.cumsum(token_counts).astype(jnp.int32)
    positions = jnp.arange(TOKENS, dtype=jnp.int32)
    request_ids = request_of(positions, request_ends)
    speeds = []
    for half in range(2):
        hidden_zero = states[half]
        normed = (layer_norm(hidden_zero) * (1.0 + request_mod(modulation, request_ids, 1)) + request_mod(modulation, request_ids, 0)).astype(jnp.bfloat16)
        query_proj = jnp.dot(normed, self_qkv[:, 0, :], preferred_element_type=jnp.float32)
        queries = rms_norm(query_proj, qk_gains[0])
        key_proj = jnp.dot(normed, self_qkv[:, 1, :], preferred_element_type=jnp.float32)
        key_rows = rms_norm(key_proj, qk_gains[1])
        value_proj = jnp.dot(normed, self_qkv[:, 2, :D], preferred_element_type=jnp.float32)
        value_rows = value_proj.astype(jnp.bfloat16)
        self_mix = pad_heads(self_attention(queries, key_rows, value_rows, request_ids))
        hidden_one = hidden_zero + request_mod(modulation, request_ids, 2) * grouped_project(self_mix, self_out)
        cross_in = (layer_norm(hidden_one) * cross_gain).astype(jnp.bfloat16)
        cross_proj = jnp.dot(cross_in, cross_query, preferred_element_type=jnp.float32)
        cross_q = rms_norm(cross_proj, qk_gains[2])
        cross_mix = pad_heads(cross_attention(cross_q, request_ids, text_kv[half], text_lens[half], qk_gains[3]))
        hidden_two = hidden_one + grouped_project(cross_mix, cross_out)
        ffn_in = (layer_norm(hidden_two) * (1.0 + request_mod(modulation, request_ids, 4)) + request_mod(modulation, request_ids, 3)).astype(jnp.bfloat16)
        hidden_three = hidden_two + request_mod(modulation, request_ids, 5) * feed_forward(ffn_in, ffn_in_weight, ffn_out_weight)
        speeds.append(jnp.dot(layer_norm(hidden_three).astype(jnp.bfloat16), head_weight, preferred_element_type=jnp.float32))
    cond_speed, plain_speed = speeds
    guided = plain_speed + guide_scale * (cond_speed - plain_speed)
    cond_sq = jax.ops.segment_sum(lax.optimization_barrier(jnp.sum(cond_speed * cond_speed, axis=1)), request_ids, REQS)
    guided_sq = jax.ops.segment_sum(lax.optimization_barrier(jnp.sum(guided * guided, axis=1)), request_ids, REQS)
    raw_peak = jax.ops.segment_max(lax.optimization_barrier(jnp.max(jnp.abs(guided), axis=1)), request_ids, REQS)
    entry_counts = token_counts.astype(jnp.float32) * OUT
    cond_rms = jnp.sqrt(cond_sq / entry_counts + stat_eps)
    guided_rms = jnp.sqrt(guided_sq / entry_counts + stat_eps)
    factor = rescale_mix * cond_rms / guided_rms + (1.0 - rescale_mix)
    step_value = steps_index.astype(jnp.float32)
    delta_t = noise_level(step_value + 1.0) - noise_level(step_value)
    velocity = factor[request_ids][:, None] * guided
    new_latent = latent + delta_t[request_ids][:, None] * velocity
    return (new_latent, velocity, factor * raw_peak)
```

```python
import functools

import jax
import jax.numpy as jnp
from jax import lax
from jax.experimental import pallas as pl
from jax.experimental.pallas import tpu as pltpu
from jax.sharding import PartitionSpec as P

HEADS = 12
HD = 128
STEPS = 50

guide_scale = 5.0
rescale_mix = 0.7
flow_shift = 5.0
norm_eps = 1e-06
stat_eps = 1e-05

MESH = pl.DeviceIdType.MESH
BF = jnp.bfloat16
F32 = jnp.float32
VMEM_LIMIT = 48 << 20


def peer_at(axis, offset):
    return lax.rem(lax.axis_index(axis) + offset, lax.axis_size(axis))


def greet(peers):
    barrier = pltpu.get_barrier_semaphore()
    for device in peers:
        pl.semaphore_signal(barrier, inc=1, device_id=device, device_id_type=MESH)
    pl.semaphore_wait(barrier, len(peers))


def others(axis):
    return [{axis: peer_at(axis, offset)} for offset in range(1, lax.axis_size(axis))]


def remote(source, target, send, recv, device):
    return pltpu.make_async_remote_copy(
        src_ref=source,
        dst_ref=target,
        send_sem=send,
        recv_sem=recv,
        device_id=device,
        device_id_type=MESH,
    )


def layer_norm(values):
    average = jnp.mean(values, axis=-1, keepdims=True)
    centered = values - average
    spread = jnp.mean(centered * centered, axis=-1, keepdims=True)
    return centered * lax.rsqrt(spread + norm_eps)


def request_bounds(counts):
    ends = []
    total = jnp.int32(0)
    for r in range(counts.shape[0]):
        total = total + counts[r]
        ends.append(total)
    return ends


def request_column(first, rows, ends):
    position = first + lax.broadcasted_iota(jnp.int32, (rows, 1), 0)
    request = jnp.zeros((rows, 1), jnp.int32)
    for end in ends[:-1]:
        request = request + jnp.where(position >= end, 1, 0)
    return request


def pick(request, choices):
    value = choices[0]
    for r in range(1, len(choices)):
        value = jnp.where(request == r, choices[r], value)
    return value


def mod_rows(mod, request, k):
    return pick(request, [mod[r, k : k + 1, :] for r in range(mod.shape[0])])


def dot(a, b):
    return jnp.dot(a, b, preferred_element_type=F32)


def dot_t(a, b):
    return lax.dot_general(a, b, (((1,), (1,)), ((), ())), preferred_element_type=F32)


def keep_columns(cols):
    if cols * lax.axis_size("tp") <= HEADS * HD:
        return None
    place = lax.axis_index("tp") * cols + lax.broadcasted_iota(jnp.int32, (1, cols), 1)
    return jnp.where(place < HEADS * HD, 1.0, 0.0).astype(F32)


def kept(values, keep):
    return values if keep is None else values * keep


def columns_to_rows(columns):
    rows = columns[0].shape[0]
    lane = lax.broadcasted_iota(jnp.int32, (rows, HD), 1)
    wide = jnp.zeros((rows, HD), F32)
    for i, column in enumerate(columns):
        wide = jnp.where(lane == i, column, wide)
    return jnp.transpose(wide)[:8]


def rows_to_columns(values):
    cols = values.shape[1]
    tall = jnp.concatenate([values, jnp.zeros((HD - 8, cols), F32)], axis=0)
    return jnp.transpose(tall)


def spread_tp(source_of, target_of, send, recv):
    copies = []
    for offset in range(1, lax.axis_size("tp")):
        copy = remote(
            source_of(offset),
            target_of(offset),
            send.at[offset],
            recv.at[offset],
            {"tp": peer_at("tp", offset)},
        )
        copy.start()
        copies.append(copy)
    return copies


def gather_tp(buffer, send, recv):
    me = lax.axis_index("tp")
    return spread_tp(lambda o: buffer.at[me], lambda o: buffer.at[me], send, recv)


def scatter_sum(mix, weight, part, landed, send, recv):
    parts = lax.axis_size("tp")
    copies = []
    for offset in list(range(1, parts)) + [0]:
        target = peer_at("tp", offset)
        part[offset] = dot(mix[target], weight[...]).astype(BF)
        if offset:
            copy = remote(
                part.at[offset],
                landed.at[offset],
                send.at[offset],
                recv.at[offset],
                {"tp": target},
            )
            copy.start()
            copies.append(copy)
    total = part[0].astype(F32)
    for offset, copy in enumerate(copies, 1):
        copy.wait_recv()
        total = total + landed[offset].astype(F32)
    for copy in copies:
        copy.wait_send()
    return total


def add_keys(query, key, value, mask, numer, denom, head):
    cols = slice(head * HD, (head + 1) * HD)
    scores = dot_t(query, key) * HD ** (-0.5)
    weights = jnp.where(mask, jnp.exp(scores), 0.0)
    lanes = denom[head]
    for start in range(0, weights.shape[1], HD):
        lanes = lanes + weights[:, start : start + HD]
    denom[head] = lanes
    numer[:, cols] = numer[:, cols] + dot(weights.astype(BF), value)


def finish(numer, denom, mix, keep):
    parts, rows, width = mix.shape
    for head in range(width // HD):
        cols = slice(head * HD, (head + 1) * HD)
        total = jnp.sum(denom[head], axis=1, keepdims=True)
        mixed = numer[:, cols] / total
        if keep is not None:
            mixed = mixed * keep[:, cols]
        mix[:, :, cols] = mixed.astype(BF).reshape(parts, rows, HD)


def self_kernel(
    counts, mod, states, qkv, gains, out_weight, hidden,
    rows_all, squares, keys, values, query, numer, denom, mix, part, landed,
    ag_send, ag_recv, sq_send, sq_recv, k_send, k_recv, v_send, v_recv, rs_send, rs_recv,
):
    greet(others("tp") + others("req"))
    rows, width = states.shape
    cols = out_weight.shape[0]
    parts, blocks = lax.axis_size("tp"), lax.axis_size("req")
    tp, req = lax.axis_index("tp"), lax.axis_index("req")
    block_rows = rows * parts
    ends = request_bounds(counts)
    request = request_column((req * parts + tp) * rows, rows, ends)
    keep = keep_columns(cols)
    rows_all[tp] = (
        layer_norm(states[...]) * (1.0 + mod_rows(mod, request, 1)) + mod_rows(mod, request, 0)
    ).astype(BF)
    pending = gather_tp(rows_all, ag_send, ag_recv)
    numer[...] = jnp.zeros_like(numer)
    denom[...] = jnp.zeros_like(denom)
    for copy in pending:
        copy.wait_recv()
    full = rows_all[...].reshape(block_rows, width)
    raw_q = kept(dot(full, qkv[:, :cols]), keep)
    raw_k = kept(dot(full, qkv[:, cols : 2 * cols]), keep)
    squares[tp] = columns_to_rows(
        [
            jnp.sum(raw_q * raw_q, axis=1, keepdims=True),
            jnp.sum(raw_k * raw_k, axis=1, keepdims=True),
        ]
    )
    square_copies = gather_tp(squares, sq_send, sq_recv)
    values[req] = dot(full, qkv[:, 2 * cols :]).astype(BF)

    def block_copy(buffer, send, recv, offset):
        return remote(
            buffer.at[req],
            buffer.at[req],
            send.at[offset],
            recv.at[offset],
            {"req": lax.rem(req + offset, blocks)},
        )

    def send_values(offset, carry):
        block_copy(values, v_send, v_recv, offset).start()
        return carry

    def send_keys(offset, carry):
        block_copy(keys, k_send, k_recv, offset).start()
        return carry

    lax.fori_loop(1, blocks, send_values, 0)
    for copy in square_copies:
        copy.wait_recv()
    sums = squares[0]
    for i in range(1, parts):
        sums = sums + squares[i]
    scale = lax.rsqrt(rows_to_columns(sums) / width + norm_eps)
    keys[req] = (raw_k * scale[:, 1:2] * gains[1:2, :]).astype(BF)
    lax.fori_loop(1, blocks, send_keys, 0)
    query[...] = (raw_q * scale[:, 0:1] * gains[0:1, :]).astype(BF)

    query_request = request_column(req * block_rows, block_rows, ends)
    lows = pick(query_request, [jnp.int32(0)] + ends[:-1])
    highs = pick(query_request, ends)

    def attend(slot):
        place = slot * block_rows + lax.broadcasted_iota(jnp.int32, (1, block_rows), 1)
        mask = (place >= lows) & (place < highs)
        for head in range(cols // HD):
            span = slice(head * HD, (head + 1) * HD)
            add_keys(
                query[:, span], keys[slot, :, span], values[slot, :, span], mask, numer, denom, head
            )

    attend(req)

    def visit(offset, carry):
        block_copy(keys, k_send, k_recv, offset).wait_recv()
        block_copy(values, v_send, v_recv, offset).wait_recv()
        attend(lax.rem(req + blocks - offset, blocks))
        return carry

    lax.fori_loop(1, blocks, visit, 0)
    finish(numer, denom, mix, keep)
    delta = scatter_sum(mix, out_weight, part, landed, rs_send, rs_recv)
    hidden[...] = states[...] + mod_rows(mod, request, 2) * delta

    def drain(offset, carry):
        block_copy(keys, k_send, k_recv, offset).wait_send()
        block_copy(values, v_send, v_recv, offset).wait_send()
        return carry

    lax.fori_loop(1, blocks, drain, 0)
    for copy in pending + square_copies:
        copy.wait_send()


def cross_kernel(
    counts, lens, states, gain, query_weight, gains, text, out_weight, hidden,
    rows_all, squares, text_squares, text_keys, numer, denom, mix, part, landed,
    ag_send, ag_recv, sq_send, sq_recv, tx_send, tx_recv, rs_send, rs_recv,
):
    greet(others("tp"))
    rows, width = states.shape
    cols = out_weight.shape[0]
    requests, slots = text.shape[0], text.shape[2]
    parts = lax.axis_size("tp")
    tp, req = lax.axis_index("tp"), lax.axis_index("req")
    block_rows = rows * parts
    ends = request_bounds(counts)
    keep = keep_columns(cols)
    rows_all[tp] = (layer_norm(states[...]) * gain[...]).astype(BF)
    pending = gather_tp(rows_all, ag_send, ag_recv)
    sums = []
    for r in range(requests):
        raw = kept(text[r, 0].astype(F32), keep)
        sums.append(jnp.sum(raw * raw, axis=1, keepdims=True))
    text_squares[tp] = columns_to_rows(sums)
    text_copies = gather_tp(text_squares, tx_send, tx_recv)
    numer[...] = jnp.zeros_like(numer)
    denom[...] = jnp.zeros_like(denom)
    for copy in text_copies:
        copy.wait_recv()
    total = text_squares[0]
    for i in range(1, parts):
        total = total + text_squares[i]
    scale = lax.rsqrt(rows_to_columns(total) / width + norm_eps)
    for r in range(requests):
        raw = kept(text[r, 0].astype(F32), keep)
        text_keys[r] = (raw * scale[:, r : r + 1] * gains[3:4, :]).astype(BF)
    for copy in pending:
        copy.wait_recv()
    raw_q = kept(dot(rows_all[...].reshape(block_rows, width), query_weight[...]), keep)
    squares[tp] = columns_to_rows([jnp.sum(raw_q * raw_q, axis=1, keepdims=True)])
    square_copies = gather_tp(squares, sq_send, sq_recv)
    for copy in square_copies:
        copy.wait_recv()
    total = squares[0]
    for i in range(1, parts):
        total = total + squares[i]
    scale = lax.rsqrt(rows_to_columns(total) / width + norm_eps)
    query = (raw_q * scale[:, 0:1] * gains[2:3, :]).astype(BF)
    query_request = request_column(req * block_rows, block_rows, ends)
    place = lax.broadcasted_iota(jnp.int32, (1, slots), 1)
    for r in range(requests):
        limit = jnp.where(query_request == r, lens[0, r], 0)
        mask = place < limit
        for head in range(cols // HD):
            span = slice(head * HD, (head + 1) * HD)
            add_keys(
                query[:, span], text_keys[r, :, span], text[r, 1, :, span], mask, numer, denom, head
            )
    finish(numer, denom, mix, keep)
    hidden[...] = states[...] + scatter_sum(mix, out_weight, part, landed, rs_send, rs_recv)
    for copy in pending + text_copies + square_copies:
        copy.wait_send()


def noise_level(step_value):
    fraction = 1.0 - step_value / STEPS
    return flow_shift * fraction / (1.0 + (flow_shift - 1.0) * fraction)


def ffn_kernel(
    chunk, counts, steps, mod, states, in_weight, out_weight, head_weight, latent,
    new_latent, velocity_out, peak_out,
    rows_all, acc, half, from_core, part, landed, speed, stats_tp, stats_req,
    ag_send, ag_recv, fw_send, fw_recv, core_send, core_recv, swap_send, swap_recv,
    rs_send, rs_recv, st_send, st_recv, sr_send, sr_recv,
):
    core, tp, req = lax.axis_index("cfg"), lax.axis_index("tp"), lax.axis_index("req")
    mate = {"cfg": 1 - core}
    greet(others("tp") + others("req") + [mate])
    rows, width = states.shape
    parts, blocks = lax.axis_size("tp"), lax.axis_size("req")
    block_rows = rows * parts
    units = in_weight.shape[0]
    requests = counts.shape[0]
    ends = request_bounds(counts)
    request = request_column((req * parts + tp) * rows, rows, ends)
    mine = rows_all.at[core]
    mine[tp] = (
        layer_norm(states[...]) * (1.0 + mod_rows(mod, request, 4)) + mod_rows(mod, request, 3)
    ).astype(BF)
    pending = gather_tp(mine, ag_send, ag_recv)
    forwards = []

    def forward(offset):
        source = lax.rem(tp + parts - offset, parts)
        copy = remote(
            rows_all.at[core, source],
            rows_all.at[core, source],
            fw_send.at[offset],
            fw_recv.at[offset],
            mate,
        )
        copy.start()
        forwards.append(copy)

    forward(0)
    for offset, copy in enumerate(pending, 1):
        copy.wait_recv()
        forward(offset)

    def work(which):
        full = rows_all[which].reshape(block_rows, width)
        acc[...] = jnp.zeros_like(acc)

        def step(i, carry):
            span = pl.ds(pl.multiple_of(i * chunk, 16), chunk)
            up = dot_t(full, in_weight[span, :])
            act = jax.nn.gelu(up, approximate=True).astype(BF)
            acc[...] = acc[...] + dot(act, out_weight[span, :])
            return carry

        lax.fori_loop(0, units // chunk, step, 0)

    for copy in forwards:
        copy.wait_recv()
    work(1 - core)
    half[...] = acc[...].astype(BF)
    across = remote(half, from_core, core_send, core_recv, mate)
    across.start()
    work(core)
    across.wait_recv()
    copies = []
    for offset in list(range(1, parts)) + [0]:
        target = peer_at("tp", offset)
        span = pl.ds(pl.multiple_of(target * rows, 16), rows)
        total = acc[span, :] + from_core[span, :].astype(F32)
        if offset:
            part[offset] = total.astype(BF)
            copy = remote(
                part.at[offset],
                landed.at[offset],
                rs_send.at[offset],
                rs_recv.at[offset],
                {"tp": target},
            )
            copy.start()
            copies.append(copy)
    for offset, copy in enumerate(copies, 1):
        copy.wait_recv()
        total = total + landed[offset].astype(F32)
    last = states[...] + mod_rows(mod, request, 5) * total
    own = dot(layer_norm(last).astype(BF), head_weight[...])
    speed[0] = own
    swap = remote(speed.at[0], speed.at[1], swap_send, swap_recv, mate)
    swap.start()
    swap.wait()
    other = speed[1]
    cond = jnp.where(core == 0, own, other)
    plain = jnp.where(core == 0, other, own)
    guided = plain + guide_scale * (cond - plain)
    lane = lax.broadcasted_iota(jnp.int32, (8, HD), 1)
    line = lax.broadcasted_iota(jnp.int32, (8, HD), 0)
    pack = jnp.zeros((8, HD), F32)
    per_row = [
        jnp.sum(cond * cond, axis=1, keepdims=True),
        jnp.sum(guided * guided, axis=1, keepdims=True),
        jnp.max(jnp.abs(guided), axis=1, keepdims=True),
    ]
    for r in range(requests):
        for i, column in enumerate(per_row):
            chosen = jnp.where(request == r, column, 0.0)
            if i < 2:
                value = jnp.sum(chosen, axis=0, keepdims=True)
            else:
                value = jnp.max(chosen, axis=0, keepdims=True)
            pack = jnp.where((lane == r) & (line == i), value, pack)

    def combine(buffer):
        total, top = buffer[0], buffer[0]
        for i in range(1, buffer.shape[0]):
            total = total + buffer[i]
            top = jnp.maximum(top, buffer[i])
        return jnp.where(line == 2, top, total)

    stats_tp[tp] = pack
    stat_copies = gather_tp(stats_tp, st_send, st_recv)
    for copy in stat_copies:
        copy.wait_recv()
    stats_req[req] = combine(stats_tp)
    for offset in range(1, blocks):
        copy = remote(
            stats_req.at[req],
            stats_req.at[req],
            sr_send.at[offset],
            sr_recv.at[offset],
            {"req": peer_at("req", offset)},
        )
        copy.start()
        stat_copies.append(copy)
    for copy in stat_copies[parts - 1 :]:
        copy.wait_recv()
    stats = combine(stats_req)
    lanes = lane[:1]
    count = jnp.ones((1, HD), F32)
    step_value = jnp.zeros((1, HD), F32)
    for r in range(requests):
        count = jnp.where(lanes == r, (counts[r] * guided.shape[1]).astype(F32), count)
        step_value = jnp.where(lanes == r, steps[r].astype(F32), step_value)
    cond_rms = jnp.sqrt(stats[0:1] / count + stat_eps)
    guided_rms = jnp.sqrt(stats[1:2] / count + stat_eps)
    factor = rescale_mix * cond_rms / guided_rms + (1.0 - rescale_mix)
    delta_t = noise_level(step_value + 1.0) - noise_level(step_value)
    peak_out[...] = factor * stats[2:3]
    row_factor = pick(request, [factor[:, r : r + 1] for r in range(requests)])
    row_step = pick(request, [delta_t[:, r : r + 1] for r in range(requests)])
    velocity = row_factor * guided
    moved = latent[...] + row_step * velocity
    own_cols = velocity_out.shape[1]
    velocity_out[...] = jnp.where(core == 0, velocity[:, :own_cols], velocity[:, own_cols:])
    new_latent[...] = jnp.where(core == 0, moved[:, :own_cols], moved[:, own_cols:])
    for copy in pending + forwards + copies + stat_copies + [across]:
        copy.wait_send()


def call(body, outs, spaces, scratch, collective, flops):
    return pl.pallas_call(
        body,
        out_shape=outs,
        in_specs=[pl.BlockSpec(memory_space=space) for space in spaces],
        out_specs=jax.tree.map(lambda _: pl.BlockSpec(memory_space=pltpu.VMEM), outs),
        scratch_shapes=scratch,
        compiler_params=pltpu.CompilerParams(
            collective_id=collective, has_side_effects=True, vmem_limit_bytes=VMEM_LIMIT
        ),
        cost_estimate=pl.CostEstimate(flops=flops, bytes_accessed=8 << 20, transcendentals=0),
    )


def shards(
    latent,
    states,
    token_counts,
    text_lens,
    steps_index,
    modulation,
    self_qkv,
    self_out,
    qk_gains,
    cross_query,
    cross_out,
    cross_gain,
    text_kv,
    ffn_in_weight,
    ffn_out_weight,
    head_weight,
):
    rows = latent.shape[0]
    width = head_weight.shape[0]
    cols = self_out.shape[0]
    heads = cols // HD
    parts, blocks = lax.axis_size("tp"), lax.axis_size("req")
    block_rows = rows * parts
    requests, slots = text_kv.shape[1], text_kv.shape[3]
    V, S = pltpu.VMEM, pltpu.SMEM

    def sems(*sizes):
        return [pltpu.SemaphoreType.DMA((size,)) for size in sizes for _ in range(2)]

    wide = pltpu.VMEM((parts, rows, width), BF)
    attention = [
        pltpu.VMEM((block_rows, cols), F32),
        pltpu.VMEM((heads, block_rows, HD), F32),
        pltpu.VMEM((parts, rows, cols), BF),
        wide,
        wide,
    ]
    hidden_shape = jax.ShapeDtypeStruct((rows, width), F32)
    hidden = call(
        self_kernel,
        hidden_shape,
        [S, V, V, V, V, V],
        [
            wide,
            pltpu.VMEM((parts, 8, block_rows), F32),
            pltpu.VMEM((blocks, block_rows, cols), BF),
            pltpu.VMEM((blocks, block_rows, cols), BF),
            pltpu.VMEM((block_rows, cols), BF),
        ]
        + attention
        + sems(parts, parts, blocks, blocks, parts),
        1,
        2 * block_rows * width * cols * 4,
    )(token_counts, modulation, states[0], self_qkv.reshape(width, 3 * cols), qk_gains, self_out)
    hidden = call(
        cross_kernel,
        hidden_shape,
        [S, S, V, V, V, V, V, V],
        [
            wide,
            pltpu.VMEM((parts, 8, block_rows), F32),
            pltpu.VMEM((parts, 8, slots), F32),
            pltpu.VMEM((requests, slots, cols), BF),
        ]
        + attention
        + sems(parts, parts, parts, parts),
        2,
        2 * block_rows * width * cols * 2,
    )(
        token_counts,
        text_lens,
        hidden,
        cross_gain.reshape(1, width),
        cross_query,
        qk_gains,
        text_kv[0],
        cross_out,
    )
    units = ffn_in_weight.shape[0]
    chunk = units // 5 if units % 80 == 0 else units
    out_cols = latent.shape[1] // lax.axis_size("cfg")
    small = jax.ShapeDtypeStruct((rows, out_cols), F32)
    new_latent, velocity, peak = call(
        functools.partial(ffn_kernel, chunk),
        (small, small, jax.ShapeDtypeStruct((1, HD), F32)),
        [S, S, V, V, V, V, V, V],
        [
            pltpu.VMEM((2, parts, rows, width), BF),
            pltpu.VMEM((block_rows, width), F32),
            pltpu.VMEM((block_rows, width), BF),
            pltpu.VMEM((block_rows, width), BF),
            wide,
            wide,
            pltpu.VMEM((2, rows, latent.shape[1]), F32),
            pltpu.VMEM((parts, 8, HD), F32),
            pltpu.VMEM((blocks, 8, HD), F32),
        ]
        + sems(parts, parts)
        + [pltpu.SemaphoreType.DMA] * 4
        + sems(parts, parts, blocks),
        3,
        4 * 2 * block_rows * width * units,
    )(
        token_counts,
        steps_index,
        modulation,
        hidden,
        ffn_in_weight,
        ffn_out_weight,
        head_weight,
        latent,
    )
    return new_latent, velocity, peak[0, :requests]


def solution(mesh):
    in_specs = (
        P(("req", "tp"), None),
        P("cfg", ("req", "tp"), None),
        P(),
        P("cfg", None),
        P(),
        P(),
        P(None, None, "tp"),
        P("tp", None),
        P(None, "tp"),
        P(None, "tp"),
        P("tp", None),
        P(),
        P("cfg", None, None, None, "tp"),
        P(("cfg", "tp"), None),
        P(("cfg", "tp"), None),
        P(),
    )
    out_specs = (P(("req", "tp"), "cfg"), P(("req", "tp"), "cfg"), P())
    return jax.shard_map(shards, mesh=mesh, in_specs=in_specs, out_specs=out_specs, check_vma=False)
```

```python
import functools
import types

import jax
import jax.numpy as jnp
from jax import lax
from jax.experimental import pallas as pl
from jax.experimental.pallas import tpu as pltpu
from jax.sharding import PartitionSpec as P

HEADS = 12
HD = 128
STEPS = 50

guide_scale = 5.0
rescale_mix = 0.7
flow_shift = 5.0
norm_eps = 1e-06
stat_eps = 1e-05

MESH = pl.DeviceIdType.MESH
BF = jnp.bfloat16
F32 = jnp.float32
VMEM_LIMIT = 60 << 20


def peer_at(axis, offset):
    return lax.rem(lax.axis_index(axis) + offset, lax.axis_size(axis))


def greet(peers):
    barrier = pltpu.get_barrier_semaphore()
    for device in peers:
        pl.semaphore_signal(barrier, inc=1, device_id=device, device_id_type=MESH)
    pl.semaphore_wait(barrier, len(peers))


def others(axis):
    return [{axis: peer_at(axis, offset)} for offset in range(1, lax.axis_size(axis))]


def remote(source, target, send, recv, device):
    return pltpu.make_async_remote_copy(
        src_ref=source,
        dst_ref=target,
        send_sem=send,
        recv_sem=recv,
        device_id=device,
        device_id_type=MESH,
    )


def layer_norm(values):
    average = jnp.mean(values, axis=-1, keepdims=True)
    centered = values - average
    spread = jnp.mean(centered * centered, axis=-1, keepdims=True)
    return centered * lax.rsqrt(spread + norm_eps)


def request_bounds(counts):
    ends = []
    total = jnp.int32(0)
    for r in range(counts.shape[0]):
        total = total + counts[r]
        ends.append(total)
    return ends


def pick(request, choices):
    value = choices[0]
    for r in range(1, len(choices)):
        value = jnp.where(request == r, choices[r], value)
    return value


def mod_rows(mod, request, k):
    return pick(request, [mod[r, k : k + 1, :] for r in range(mod.shape[0])])


def dot(a, b):
    return jnp.dot(a, b, preferred_element_type=F32)


def dot_t(a, b):
    return lax.dot_general(a, b, (((1,), (1,)), ((), ())), preferred_element_type=F32)


def keep_columns(cols):
    if cols * lax.axis_size("tp") <= HEADS * HD:
        return None
    place = lax.axis_index("tp") * cols + lax.broadcasted_iota(jnp.int32, (1, cols), 1)
    return jnp.where(place < HEADS * HD, 1.0, 0.0).astype(F32)


def kept(values, keep):
    return values if keep is None else values * keep


def columns_to_rows(columns):
    rows = columns[0].shape[0]
    lane = lax.broadcasted_iota(jnp.int32, (rows, HD), 1)
    wide = jnp.zeros((rows, HD), F32)
    for i, column in enumerate(columns):
        wide = jnp.where(lane == i, column, wide)
    return jnp.transpose(wide)[:8]


def rows_to_columns(values):
    cols = values.shape[1]
    tall = jnp.concatenate([values, jnp.zeros((HD - 8, cols), F32)], axis=0)
    return jnp.transpose(tall)


class Gather:
    def __init__(self, buffer, send, recv, chunk, relayed=False):
        self.tp, self.parts = lax.axis_index("tp"), lax.axis_size("tp")
        self.line = relayed and self.parts == 4
        self.inner = (self.tp == 1) | (self.tp == 2)
        self.buffer, self.send, self.recv, self.chunk = buffer, send, recv, chunk
        self.copies = {o: self.copy(self.tp, o) for o in range(1, self.parts)}
        self.onward = None
        for offset in sorted(self.copies, key=lambda o: (o != 2, o)):
            self.unless(self.line and self.skips_send(offset), self.copies[offset].start)

    def copy(self, source, offset):
        return remote(
            self.buffer.at[source],
            self.buffer.at[source],
            self.send.at[self.chunk, offset],
            self.recv.at[self.chunk, offset],
            {"tp": lax.rem(self.tp + offset, self.parts)},
        )

    def skips_send(self, offset):
        return {1: self.tp == 3, 3: self.tp == 0}.get(offset, False)

    def unless(self, condition, action):
        if condition is False:
            action()
        else:
            pl.when(jnp.logical_not(condition))(action)

    def relay(self):
        if not self.line or self.onward is not None:
            return
        source = 3 * (2 - self.tp)
        self.onward = remote(
            self.buffer.at[source],
            self.buffer.at[source],
            self.send.at[self.chunk, 0],
            self.recv.at[self.chunk, 2 * self.tp - 1],
            {"tp": 3 * (self.tp - 1)},
        )

        @pl.when(self.inner)
        def _():
            self.copies[2].wait_recv()
            self.onward.start()

    def wait_one(self, offset):
        self.relay()
        skip = self.inner if self.line and offset == 2 else False
        self.unless(skip, self.copies[offset].wait_recv)

    def wait_recv(self):
        for offset in self.copies:
            self.wait_one(offset)

    def wait_send(self):
        for offset, copy in self.copies.items():
            self.unless(self.line and self.skips_send(offset), copy.wait_send)
        if self.line:
            pl.when(self.inner)(self.onward.wait_send)


class Scatter:
    def __init__(self, part, landed, send, recv, chunk):
        self.tp, self.parts = lax.axis_index("tp"), lax.axis_size("tp")
        self.line = self.parts == 4
        self.inner = (self.tp == 1) | (self.tp == 2)
        self.part, self.landed = part, landed
        self.copies, self.vias, self.relayed = {}, {}, False
        self.first = None
        for offset in sorted(range(1, self.parts), key=lambda o: (o == 2, -o)):
            target = lax.rem(self.tp + offset, self.parts)
            copy = remote(
                part.at[target],
                landed.at[offset],
                send.at[chunk, offset],
                recv.at[chunk, offset],
                {"tp": target},
            )
            self.copies[offset] = copy
            if not self.line:
                copy.start()
            elif offset == 2:
                pl.when(jnp.logical_not(self.inner))(copy.start)
            else:
                far = self.far(offset)
                via = remote(
                    part.at[target],
                    landed.at[0],
                    send.at[chunk, offset],
                    recv.at[chunk, 0],
                    {"tp": 1 if offset == 3 else 2},
                )
                self.vias[offset] = via
                pl.when(far)(via.start)
                pl.when(jnp.logical_not(far))(copy.start)

    def far(self, offset):
        return self.tp == (0 if offset == 3 else 3)

    def relay(self):
        if not self.line or self.relayed:
            return
        self.relayed = True
        target = lax.rem(self.tp + 2, self.parts)

        @pl.when(self.inner)
        def _():
            self.vias[3].wait_recv()
            joined = self.part[target].astype(F32) + self.landed[0].astype(F32)
            self.part[target] = joined.astype(BF)
            self.copies[2].start()

        for offset in (1, 3):

            @pl.when(self.tp == (0 if offset == 1 else 3))
            def _(offset=offset):
                self.landed[offset] = jnp.zeros(self.landed.shape[1:], BF)

    def total(self):
        self.relay()
        total = self.part[self.tp].astype(F32)
        for offset in sorted(self.copies):
            wait = self.copies[offset].wait_recv
            if self.line and offset != 2:
                pl.when(self.tp != (0 if offset == 1 else 3))(wait)
            else:
                wait()
            total = total + self.landed[offset].astype(F32)
        return total

    def wait_send(self):
        for copy in self.copies.values():
            copy.wait_send()


def placed(index, segments):
    place = index
    for start, first in segments:
        place = jnp.where(index >= start, index - start + first, place)
    return place


def request_at(position, ends):
    request = jnp.zeros(position.shape, jnp.int32)
    for end in ends[:-1]:
        request = request + jnp.where(position >= end, 1, 0)
    return request


def add_all(buffer):
    total = buffer[0]
    for i in range(1, buffer.shape[0]):
        total = total + buffer[i]
    return total


def row_scale(squares, width):
    return lax.rsqrt(rows_to_columns(add_all(squares)) / width + norm_eps)


def square_sums(values):
    return jnp.sum(values * values, axis=1, keepdims=True)


def add_keys(query, key, value, mask, numer, denom, head, first=0):
    rows = slice(first, first + query.shape[0])
    cols = slice(head * HD, (head + 1) * HD)
    scores = dot_t(query, key) * HD ** (-0.5)
    weights = jnp.where(mask, jnp.exp(scores), 0.0)
    lanes = denom[head, rows, :]
    for start in range(0, weights.shape[1], HD):
        lanes = lanes + weights[:, start : start + HD]
    denom[head, rows, :] = lanes
    numer[rows, cols] = numer[rows, cols] + dot(weights.astype(BF), value)


def finish(numer, denom, mix, keep, first):
    parts, size, width = mix.shape
    rows = slice(first, first + parts * size)
    for head in range(width // HD):
        cols = slice(head * HD, (head + 1) * HD)
        total = jnp.sum(denom[head, rows, :], axis=1, keepdims=True)
        mixed = numer[rows, cols] / total
        if keep is not None:
            mixed = mixed * keep[:, cols]
        mix[:, :, cols] = mixed.astype(BF).reshape(parts, size, HD)


def noise_level(step_value):
    fraction = 1.0 - step_value / STEPS
    return flow_shift * fraction / (1.0 + (flow_shift - 1.0) * fraction)


def block_kernel(
    sizes, chunk_units, names, chunk_names, *refs,
):
    ref = types.SimpleNamespace(**dict(zip(names, refs)))
    rest = refs[len(names) :]
    per = []
    for c in range(len(sizes)):
        mine = rest[c * len(chunk_names) : (c + 1) * len(chunk_names)]
        per.append(types.SimpleNamespace(**dict(zip(chunk_names, mine, strict=True))))
    counts, lens, steps, mod, states = ref.counts, ref.lens, ref.steps, ref.mod, ref.states
    gains = ref.gains
    rows, width = states.shape
    cols = ref.self_out.shape[0]
    core, tp, req = lax.axis_index("cfg"), lax.axis_index("tp"), lax.axis_index("req")
    parts, blocks = lax.axis_size("tp"), lax.axis_size("req")
    block_rows = rows * parts
    heads = cols // HD
    requests = counts.shape[0]
    mate = {"cfg": 1 - core}

    def fetch(i, source, target):
        copy = pltpu.make_async_copy(source, target, ref.fetch_sem.at[i])
        copy.start()
        return copy

    fetches = types.SimpleNamespace(
        qkv=fetch(0, ref.qkv, ref.v_qkv),
        text=fetch(1, ref.text, ref.v_text),
        self_out=fetch(2, ref.self_out, ref.v_self_out),
        cross_query=fetch(3, ref.cross_query, ref.v_cross_query),
        cross_out=fetch(4, ref.cross_out, ref.v_cross_out),
        ffn_in=fetch(5, ref.ffn_in, ref.v_ffn_in),
        ffn_out=fetch(6, ref.ffn_out, ref.v_ffn_out),
    )
    greet(others("tp") + others("req") + [mate])

    starts = [sum(sizes[:c]) for c in range(len(sizes))]
    chunks = range(len(sizes))
    spans = [slice(starts[c], starts[c] + sizes[c]) for c in chunks]
    key_starts = [parts * start for start in starts]
    segments = [
        [(t * sizes[c], t * rows + starts[c]) for t in range(parts)] for c in chunks
    ]
    all_segments = [
        (key_starts[c] + start, first) for c in chunks for start, first in segments[c]
    ]
    ends = request_bounds(counts)
    row_first = (req * parts + tp) * rows
    request = [
        request_at(
            row_first + starts[c] + lax.broadcasted_iota(jnp.int32, (sizes[c], 1), 0), ends
        )
        for c in chunks
    ]
    keep = keep_columns(cols)
    done = []

    rows_self = [per[c].rows_self for c in chunks]
    gathers = []
    for c in chunks:
        rows_self[c][tp] = (
            layer_norm(states[spans[c], :]) * (1.0 + mod_rows(mod, request[c], 1))
            + mod_rows(mod, request[c], 0)
        ).astype(BF)
        gathers.append(Gather(rows_self[c], ref.ag_send, ref.ag_recv, c, True))
    numer, denom = ref.numer, ref.denom
    numer[...] = jnp.zeros_like(numer)
    denom[...] = jnp.zeros_like(denom)

    fetches.text.wait()
    text, text_squares, text_keys = ref.v_text, ref.text_squares, ref.text_keys
    text_squares[tp] = columns_to_rows(
        [square_sums(kept(text[r, 0].astype(F32), keep)) for r in range(requests)]
    )
    text_copies = Gather(text_squares, ref.tx_send, ref.tx_recv, 0)

    fetches.qkv.wait()
    qkv, keys, values, query = ref.v_qkv, ref.keys, ref.values, ref.query

    def block_copy(buffer, send, recv, c, offset):
        span = pl.ds(key_starts[c], parts * sizes[c])
        return remote(
            buffer.at[req, span],
            buffer.at[req, span],
            send.at[c, offset],
            recv.at[c, offset],
            {"req": lax.rem(req + offset, blocks)},
        )

    def key_copy(c, offset):
        return block_copy(keys, ref.k_send, ref.k_recv, c, offset)

    def value_copy(c, offset):
        return block_copy(values, ref.v_send, ref.v_recv, c, offset)

    def start_all(make, c):
        def body(offset, carry):
            make(c, offset).start()
            return carry

        lax.fori_loop(1, blocks, body, 0)

    raws, square_copies = [], []
    for c in chunks:
        gathers[c].wait_recv()
        full = rows_self[c][...].reshape(parts * sizes[c], width)
        key_span = slice(key_starts[c], key_starts[c] + parts * sizes[c])
        values[req, key_span, :] = dot(full, qkv[2]).astype(BF)
        start_all(value_copy, c)
        for later in gathers[c + 1 :]:
            later.relay()
        raw_k = kept(dot(full, qkv[1]), keep)
        raw_q = kept(dot(full, qkv[0]), keep)
        ref.raw_k[key_span, :] = raw_k
        ref.raw_q[key_span, :] = raw_q
        squares = per[c].squares_self
        squares[tp] = columns_to_rows([square_sums(raw_q), square_sums(raw_k)])
        square_copies.append(Gather(squares, ref.sq_send, ref.sq_recv, c))
    for c in chunks:
        square_copies[c].wait_recv()
        key_span = slice(key_starts[c], key_starts[c] + parts * sizes[c])
        scale = row_scale(per[c].squares_self, width)
        keys[req, key_span, :] = (ref.raw_k[key_span, :] * scale[:, 1:2] * gains[1:2, :]).astype(BF)
        start_all(key_copy, c)
        query[key_span, :] = (ref.raw_q[key_span, :] * scale[:, 0:1] * gains[0:1, :]).astype(BF)
    done += gathers + square_copies

    key_place = placed(lax.broadcasted_iota(jnp.int32, (1, block_rows), 1), all_segments)
    query_request = request_at(
        req * block_rows
        + placed(lax.broadcasted_iota(jnp.int32, (block_rows, 1), 0), all_segments),
        ends,
    )
    lows = pick(query_request, [jnp.int32(0)] + ends[:-1])
    highs = pick(query_request, ends)

    def attend(slot):
        place = slot * block_rows + key_place
        mask = (place >= lows) & (place < highs)
        for head in range(heads):
            span = slice(head * HD, (head + 1) * HD)
            add_keys(
                query[:, span], keys[slot, :, span], values[slot, :, span], mask, numer, denom, head
            )

    attend(req)
    text_copies.wait_recv()
    done.append(text_copies)
    scale = row_scale(text_squares, width)
    for r in range(requests):
        raw = kept(text[r, 0].astype(F32), keep)
        text_keys[r] = (raw * scale[:, r : r + 1] * gains[3:4, :]).astype(BF)

    def visit(offset, carry):
        for c in chunks:
            value_copy(c, offset).wait_recv()
            key_copy(c, offset).wait_recv()
        attend(lax.rem(req + blocks - offset, blocks))
        return carry

    lax.fori_loop(1, blocks, visit, 0)

    fetches.self_out.wait()
    mixes = [per[c].mix for c in chunks]

    def project(c, weight, part):
        flat = mixes[c][...].reshape(parts * sizes[c], cols)
        part[...] = dot(flat, weight[...]).astype(BF).reshape(part.shape)

    scatters = []
    for c in chunks:
        finish(numer, denom, mixes[c], keep, key_starts[c])
        project(c, ref.v_self_out, per[c].part_self)
        scatters.append(
            Scatter(per[c].part_self, per[c].landed_self, ref.rs_self_send, ref.rs_self_recv, c)
        )

    rows_cross = [per[c].rows_cross for c in chunks]
    hidden, gathers = [], []
    for item in scatters:
        item.relay()
    for c in chunks:
        delta = scatters[c].total()
        hidden_one = states[spans[c], :] + mod_rows(mod, request[c], 2) * delta
        ref.hidden[spans[c], :] = hidden_one
        rows_cross[c][tp] = (layer_norm(hidden_one) * ref.cross_gain[...]).astype(BF)
        gathers.append(Gather(rows_cross[c], ref.cg_send, ref.cg_recv, c, True))
        done += [scatters[c], gathers[c]]
    numer[...] = jnp.zeros_like(numer)
    denom[...] = jnp.zeros_like(denom)
    fetches.cross_query.wait()
    fetches.cross_out.wait()
    slots = text.shape[2]
    text_place = lax.broadcasted_iota(jnp.int32, (1, slots), 1)
    scatters = []
    for c in chunks:
        gathers[c].wait_recv()
        count = parts * sizes[c]
        raw_q = kept(dot(rows_cross[c][...].reshape(count, width), ref.v_cross_query[...]), keep)
        squares = per[c].squares_cross
        squares[tp] = columns_to_rows([square_sums(raw_q)])
        copies = Gather(squares, ref.cs_send, ref.cs_recv, c)
        done.append(copies)
        for earlier in scatters:
            earlier.relay()
        for later in gathers[c + 1 :]:
            later.relay()
        copies.wait_recv()
        scale = row_scale(squares, width)
        cross_q = (raw_q * scale[:, 0:1] * gains[2:3, :]).astype(BF)
        query_request = request_at(
            req * block_rows
            + placed(lax.broadcasted_iota(jnp.int32, (count, 1), 0), segments[c]),
            ends,
        )
        for r in range(requests):
            mask = text_place < jnp.where(query_request == r, lens[0, r], 0)
            for head in range(heads):
                span = slice(head * HD, (head + 1) * HD)
                add_keys(
                    cross_q[:, span],
                    text_keys[r, :, span],
                    text[r, 1, :, span],
                    mask,
                    numer,
                    denom,
                    head,
                    key_starts[c],
                )
        finish(numer, denom, mixes[c], keep, key_starts[c])
        project(c, ref.v_cross_out, per[c].part_cross)
        scatters.append(
            Scatter(per[c].part_cross, per[c].landed_cross, ref.rs_cross_send, ref.rs_cross_recv, c)
        )

    rows_ffn = [per[c].rows_ffn for c in chunks]
    gathers = []
    for item in scatters:
        item.relay()
    for c in chunks:
        delta = scatters[c].total()
        hidden_two = ref.hidden[spans[c], :] + delta
        ref.hidden[spans[c], :] = hidden_two
        rows_ffn[c][core, tp] = (
            layer_norm(hidden_two) * (1.0 + mod_rows(mod, request[c], 4))
            + mod_rows(mod, request[c], 3)
        ).astype(BF)
        gathers.append(Gather(rows_ffn[c].at[core], ref.fg_send, ref.fg_recv, c, True))
        done += [scatters[c], gathers[c]]

    def forward(c, offset):
        view = rows_ffn[c].at[core, lax.rem(tp + parts - offset, parts)]
        copy = remote(view, view, ref.fw_send.at[c, offset], ref.fw_recv.at[c, offset], mate)
        copy.start()
        return copy

    forwards = [[forward(c, 0)] for c in chunks]

    def forward_rest(c):
        gathers[c].relay()
        for offset in gathers[c].copies:
            gathers[c].wait_one(offset)
            forwards[c].append(forward(c, offset))

    fetches.ffn_in.wait()
    fetches.ffn_out.wait()
    scatters = []
    forward_rest(0)
    for c in chunks:
        count = parts * sizes[c]
        acc, half, from_core = per[c].acc, per[c].half, per[c].from_core
        for copy in forwards[c]:
            copy.wait_recv()
        full = rows_ffn[c][...].reshape(2 * count, width)
        acc[...] = jnp.zeros_like(acc)

        def step(i, carry, full=full, acc=acc, count=count):
            span = pl.ds(pl.multiple_of(i * chunk_units, 16), chunk_units)
            up = dot_t(full, ref.v_ffn_in[span, :])
            act = jax.nn.gelu(up, approximate=True).astype(BF)
            acc[...] = acc[...] + dot(act, ref.v_ffn_out[span, :]).reshape(2, count, width)
            return carry

        loops = ref.v_ffn_in.shape[0] // chunk_units
        pause = min(2, loops)
        lax.fori_loop(0, pause, step, 0)
        for earlier in scatters:
            earlier.relay()
        for later in gathers[c + 1 :]:
            later.relay()
        lax.fori_loop(pause, loops, step, 0)
        half[...] = acc[1 - core].astype(BF)
        across = remote(half, from_core, ref.core_send.at[c], ref.core_recv.at[c], mate)
        across.start()
        if c + 1 < len(sizes):
            forward_rest(c + 1)
        across.wait_recv()

        total = acc[core] + from_core[...].astype(F32)
        per[c].part_ffn[...] = total.astype(BF).reshape(per[c].part_ffn.shape)
        scatters.append(
            Scatter(per[c].part_ffn, per[c].landed_ffn, ref.rs_ffn_send, ref.rs_ffn_recv, c)
        )
        done += forwards[c] + [across, scatters[c]]

    speed = ref.speed
    for item in scatters:
        item.relay()
    for c in chunks:
        delta = scatters[c].total()
        last = ref.hidden[spans[c], :] + mod_rows(mod, request[c], 5) * delta
        speed[0, spans[c], :] = dot_t(layer_norm(last).astype(BF), ref.head[...])
    swap = remote(speed.at[0], speed.at[1], ref.swap_send, ref.swap_recv, mate)
    swap.start()
    swap.wait_recv()
    done.append(swap)
    own, other = speed[0], speed[1]
    request = request_at(row_first + lax.broadcasted_iota(jnp.int32, (rows, 1), 0), ends)
    cond = jnp.where(core == 0, own, other)
    plain = jnp.where(core == 0, other, own)
    guided = plain + guide_scale * (cond - plain)
    lane = lax.broadcasted_iota(jnp.int32, (8, HD), 1)
    line = lax.broadcasted_iota(jnp.int32, (8, HD), 0)
    pack = jnp.zeros((8, HD), F32)
    per_row = [
        jnp.sum(cond * cond, axis=1, keepdims=True),
        jnp.sum(guided * guided, axis=1, keepdims=True),
        jnp.max(jnp.abs(guided), axis=1, keepdims=True),
    ]
    for r in range(requests):
        for i, column in enumerate(per_row):
            chosen = jnp.where(request == r, column, 0.0)
            if i < 2:
                value = jnp.sum(chosen, axis=0, keepdims=True)
            else:
                value = jnp.max(chosen, axis=0, keepdims=True)
            pack = jnp.where((lane == r) & (line == i), value, pack)

    def combine(buffer):
        total, top = buffer[0], buffer[0]
        for i in range(1, buffer.shape[0]):
            total = total + buffer[i]
            top = jnp.maximum(top, buffer[i])
        return jnp.where(line == 2, top, total)

    stats_tp, stats_req = ref.stats_tp, ref.stats_req
    stats_tp[tp] = pack
    stat_copies = [Gather(stats_tp, ref.st_send, ref.st_recv, 0)]
    stat_copies[0].wait_recv()
    stats_req[req] = combine(stats_tp)
    for offset in range(1, blocks):
        copy = remote(
            stats_req.at[req],
            stats_req.at[req],
            ref.sr_send.at[offset],
            ref.sr_recv.at[offset],
            {"req": peer_at("req", offset)},
        )
        copy.start()
        stat_copies.append(copy)
    for copy in stat_copies[1:]:
        copy.wait_recv()
    stats = combine(stats_req)
    lanes = lane[:1]
    count = jnp.ones((1, HD), F32)
    step_value = jnp.zeros((1, HD), F32)
    for r in range(requests):
        count = jnp.where(lanes == r, (counts[r] * guided.shape[1]).astype(F32), count)
        step_value = jnp.where(lanes == r, steps[r].astype(F32), step_value)
    cond_rms = jnp.sqrt(stats[0:1] / count + stat_eps)
    guided_rms = jnp.sqrt(stats[1:2] / count + stat_eps)
    factor = rescale_mix * cond_rms / guided_rms + (1.0 - rescale_mix)
    delta_t = noise_level(step_value + 1.0) - noise_level(step_value)
    ref.peak[...] = factor * stats[2:3]
    row_factor = pick(request, [factor[:, r : r + 1] for r in range(requests)])
    row_step = pick(request, [delta_t[:, r : r + 1] for r in range(requests)])
    velocity = row_factor * guided
    moved = ref.latent[...] + row_step * velocity
    new_latent, velocity_out = ref.new_latent, ref.velocity
    own_cols = velocity_out.shape[1]
    velocity_out[...] = jnp.where(core == 0, velocity[:, :own_cols], velocity[:, own_cols:])
    new_latent[...] = jnp.where(core == 0, moved[:, :own_cols], moved[:, own_cols:])
    for copy in done + stat_copies:
        copy.wait_send()

    def drain(offset, carry):
        for c in chunks:
            key_copy(c, offset).wait_send()
            value_copy(c, offset).wait_send()
        return carry

    lax.fori_loop(1, blocks, drain, 0)


def shards(
    latent,
    states,
    token_counts,
    text_lens,
    steps_index,
    modulation,
    self_qkv,
    self_out,
    qk_gains,
    cross_query,
    cross_out,
    cross_gain,
    text_kv,
    ffn_in_weight,
    ffn_out_weight,
    head_weight,
):
    rows = latent.shape[0]
    width = head_weight.shape[0]
    cols = self_out.shape[0]
    heads = cols // HD
    parts, blocks = lax.axis_size("tp"), lax.axis_size("req")
    block_rows = rows * parts
    requests, slots = text_kv.shape[1], text_kv.shape[3]
    units = ffn_in_weight.shape[0]
    chunk_units = units // 5 if units % 80 == 0 else units
    first = -(-rows // 32) * 16
    sizes = (first, rows - first)
    V, S, H = pltpu.VMEM, pltpu.SMEM, pl.ANY
    operands = dict(
        counts=(S, token_counts),
        lens=(S, text_lens),
        steps=(S, steps_index),
        mod=(V, modulation),
        states=(V, states[0]),
        gains=(V, qk_gains),
        cross_gain=(V, cross_gain.reshape(1, width)),
        head=(V, jnp.transpose(head_weight)),
        latent=(V, latent),
        qkv=(H, jnp.transpose(self_qkv, (1, 0, 2))),
        text=(H, text_kv[0]),
        self_out=(H, self_out),
        cross_query=(H, cross_query),
        cross_out=(H, cross_out),
        ffn_in=(H, ffn_in_weight),
        ffn_out=(H, ffn_out_weight),
    )
    small = jax.ShapeDtypeStruct((rows, latent.shape[1] // lax.axis_size("cfg")), F32)
    results = dict(new_latent=small, velocity=small, peak=jax.ShapeDtypeStruct((1, HD), F32))

    def sem(*shape):
        return pltpu.SemaphoreType.DMA(shape) if shape else pltpu.SemaphoreType.DMA

    two = len(sizes)
    by_tp, by_req = sem(two, parts), sem(two, blocks)
    scratch = dict(
        v_qkv=V((3, width, cols), BF),
        v_text=V(text_kv.shape[1:], BF),
        v_self_out=V(self_out.shape, BF),
        v_cross_query=V(cross_query.shape, BF),
        v_cross_out=V(cross_out.shape, BF),
        v_ffn_in=V(ffn_in_weight.shape, BF),
        v_ffn_out=V(ffn_out_weight.shape, BF),
        fetch_sem=sem(7),
        keys=V((blocks, block_rows, cols), BF),
        values=V((blocks, block_rows, cols), BF),
        query=V((block_rows, cols), BF),
        raw_q=V((block_rows, cols), F32),
        raw_k=V((block_rows, cols), F32),
        numer=V((block_rows, cols), F32),
        denom=V((heads, block_rows, HD), F32),
        text_squares=V((parts, 8, slots), F32),
        text_keys=V((requests, slots, cols), BF),
        hidden=V((rows, width), F32),
        speed=V((2, rows, latent.shape[1]), F32),
        stats_tp=V((parts, 8, HD), F32),
        stats_req=V((blocks, 8, HD), F32),
        ag_send=by_tp, ag_recv=by_tp,
        sq_send=by_tp, sq_recv=by_tp,
        tx_send=by_tp, tx_recv=by_tp,
        k_send=by_req, k_recv=by_req,
        v_send=by_req, v_recv=by_req,
        rs_self_send=by_tp, rs_self_recv=by_tp,
        cg_send=by_tp, cg_recv=by_tp,
        cs_send=by_tp, cs_recv=by_tp,
        rs_cross_send=by_tp, rs_cross_recv=by_tp,
        fg_send=by_tp, fg_recv=by_tp,
        fw_send=by_tp, fw_recv=by_tp,
        core_send=sem(two), core_recv=sem(two),
        rs_ffn_send=by_tp, rs_ffn_recv=by_tp,
        swap_send=sem(), swap_recv=sem(),
        st_send=by_tp, st_recv=by_tp,
        sr_send=sem(blocks), sr_recv=sem(blocks),
    )

    def chunk_scratch(size):
        count = parts * size
        wide = V((parts, size, width), BF)
        return dict(
            rows_self=wide, rows_cross=wide, rows_ffn=V((2, parts, size, width), BF),
            part_self=wide, landed_self=wide,
            part_cross=wide, landed_cross=wide,
            part_ffn=wide, landed_ffn=wide,
            squares_self=V((parts, 8, count), F32),
            squares_cross=V((parts, 8, count), F32),
            mix=V((parts, size, cols), BF),
            acc=V((2, count, width), F32),
            half=V((count, width), BF),
            from_core=V((count, width), BF),
        )

    chunk_dicts = [chunk_scratch(size) for size in sizes]
    names = tuple(operands) + tuple(results) + tuple(scratch)
    shapes = list(scratch.values()) + [v for d in chunk_dicts for v in d.values()]
    new_latent, velocity, peak = pl.pallas_call(
        functools.partial(block_kernel, sizes, chunk_units, names, tuple(chunk_dicts[0])),
        out_shape=tuple(results.values()),
        in_specs=[pl.BlockSpec(memory_space=space) for space, _ in operands.values()],
        out_specs=tuple(pl.BlockSpec(memory_space=V) for _ in results),
        scratch_shapes=shapes,
        compiler_params=pltpu.CompilerParams(
            collective_id=0, has_side_effects=True, vmem_limit_bytes=VMEM_LIMIT
        ),
        cost_estimate=pl.CostEstimate(
            flops=16 * block_rows * width * units, bytes_accessed=20 << 20, transcendentals=0
        ),
    )(*[value for _, value in operands.values()])
    return new_latent, velocity, peak[0, :requests]


def solution(mesh):
    in_specs = (
        P(("req", "tp"), None),
        P("cfg", ("req", "tp"), None),
        P(),
        P("cfg", None),
        P(),
        P(),
        P(None, None, "tp"),
        P("tp", None),
        P(None, "tp"),
        P(None, "tp"),
        P("tp", None),
        P(),
        P("cfg", None, None, None, "tp"),
        P(("cfg", "tp"), None),
        P(("cfg", "tp"), None),
        P(),
    )
    out_specs = (P(("req", "tp"), "cfg"), P(("req", "tp"), "cfg"), P())
    return jax.shard_map(shards, mesh=mesh, in_specs=in_specs, out_specs=out_specs, check_vma=False)
```

```python
import functools
import types

import jax
import jax.numpy as jnp
from jax import lax
from jax.experimental import pallas as pl
from jax.experimental.pallas import tpu as pltpu
from jax.sharding import PartitionSpec as P

HEADS = 12
HD = 128
STEPS = 50

guide_scale = 5.0
rescale_mix = 0.7
flow_shift = 5.0
norm_eps = 1e-06
stat_eps = 1e-05

MESH = pl.DeviceIdType.MESH
BF = jnp.bfloat16
F32 = jnp.float32
VMEM_LIMIT = 60 << 20


def peer_at(axis, offset):
    return lax.rem(lax.axis_index(axis) + offset, lax.axis_size(axis))


def greet(peers):
    barrier = pltpu.get_barrier_semaphore()
    for device in peers:
        pl.semaphore_signal(barrier, inc=1, device_id=device, device_id_type=MESH)
    pl.semaphore_wait(barrier, len(peers))


def others(axis):
    return [{axis: peer_at(axis, offset)} for offset in range(1, lax.axis_size(axis))]


def remote(source, target, send, recv, device):
    return pltpu.make_async_remote_copy(
        src_ref=source,
        dst_ref=target,
        send_sem=send,
        recv_sem=recv,
        device_id=device,
        device_id_type=MESH,
    )


def layer_norm(values):
    average = jnp.mean(values, axis=-1, keepdims=True)
    centered = values - average
    spread = jnp.mean(centered * centered, axis=-1, keepdims=True)
    return centered * lax.rsqrt(spread + norm_eps)


def request_bounds(counts):
    ends = []
    total = jnp.int32(0)
    for r in range(counts.shape[0]):
        total = total + counts[r]
        ends.append(total)
    return ends


def pick(request, choices):
    value = choices[0]
    for r in range(1, len(choices)):
        value = jnp.where(request == r, choices[r], value)
    return value


def mod_rows(mod, request, k):
    return pick(request, [mod[r, k : k + 1, :] for r in range(mod.shape[0])])


def dot(a, b):
    return jnp.dot(a, b, preferred_element_type=F32)


def dot_t(a, b):
    return lax.dot_general(a, b, (((1,), (1,)), ((), ())), preferred_element_type=F32)


def keep_columns(cols):
    if cols * lax.axis_size("tp") <= HEADS * HD:
        return None
    place = lax.axis_index("tp") * cols + lax.broadcasted_iota(jnp.int32, (1, cols), 1)
    return jnp.where(place < HEADS * HD, 1.0, 0.0).astype(F32)


def kept(values, keep):
    return values if keep is None else values * keep


def columns_to_rows(columns):
    rows = columns[0].shape[0]
    lane = lax.broadcasted_iota(jnp.int32, (rows, HD), 1)
    wide = jnp.zeros((rows, HD), F32)
    for i, column in enumerate(columns):
        wide = jnp.where(lane == i, column, wide)
    return jnp.transpose(wide)[:8]


def rows_to_columns(values):
    cols = values.shape[1]
    tall = jnp.concatenate([values, jnp.zeros((HD - 8, cols), F32)], axis=0)
    return jnp.transpose(tall)


class Gather:
    def __init__(self, buffer, send, recv, chunk, relayed=False):
        self.tp, self.parts = lax.axis_index("tp"), lax.axis_size("tp")
        self.line = relayed and self.parts == 4
        self.inner = (self.tp == 1) | (self.tp == 2)
        self.buffer, self.send, self.recv, self.chunk = buffer, send, recv, chunk
        self.copies = {o: self.copy(self.tp, o) for o in range(1, self.parts)}
        self.onward = None
        for offset in sorted(self.copies, key=lambda o: (o != 2, o)):
            self.unless(self.line and self.skips_send(offset), self.copies[offset].start)

    def copy(self, source, offset):
        return remote(
            self.buffer.at[source],
            self.buffer.at[source],
            self.send.at[self.chunk, offset],
            self.recv.at[self.chunk, offset],
            {"tp": lax.rem(self.tp + offset, self.parts)},
        )

    def skips_send(self, offset):
        return {1: self.tp == 3, 3: self.tp == 0}.get(offset, False)

    def unless(self, condition, action):
        if condition is False:
            action()
        else:
            pl.when(jnp.logical_not(condition))(action)

    def relay(self):
        if not self.line or self.onward is not None:
            return
        source = 3 * (2 - self.tp)
        self.onward = remote(
            self.buffer.at[source],
            self.buffer.at[source],
            self.send.at[self.chunk, 0],
            self.recv.at[self.chunk, 2 * self.tp - 1],
            {"tp": 3 * (self.tp - 1)},
        )

        @pl.when(self.inner)
        def _():
            self.copies[2].wait_recv()
            self.onward.start()

    def wait_one(self, offset):
        self.relay()
        skip = self.inner if self.line and offset == 2 else False
        self.unless(skip, self.copies[offset].wait_recv)

    def wait_recv(self):
        for offset in self.copies:
            self.wait_one(offset)

    def wait_send(self):
        for offset, copy in self.copies.items():
            self.unless(self.line and self.skips_send(offset), copy.wait_send)
        if self.line:
            pl.when(self.inner)(self.onward.wait_send)


class Scatter:
    def __init__(self, part, landed, send, recv, chunk):
        self.tp, self.parts = lax.axis_index("tp"), lax.axis_size("tp")
        self.line = self.parts == 4
        self.inner = (self.tp == 1) | (self.tp == 2)
        self.part, self.landed = part, landed
        self.copies, self.vias, self.relayed = {}, {}, False
        self.first = None
        for offset in sorted(range(1, self.parts), key=lambda o: (o == 2, -o)):
            target = lax.rem(self.tp + offset, self.parts)
            copy = remote(
                part.at[target],
                landed.at[offset],
                send.at[chunk, offset],
                recv.at[chunk, offset],
                {"tp": target},
            )
            self.copies[offset] = copy
            if not self.line:
                copy.start()
            elif offset == 2:
                pl.when(jnp.logical_not(self.inner))(copy.start)
            else:
                far = self.far(offset)
                via = remote(
                    part.at[target],
                    landed.at[0],
                    send.at[chunk, offset],
                    recv.at[chunk, 0],
                    {"tp": 1 if offset == 3 else 2},
                )
                self.vias[offset] = via
                pl.when(far)(via.start)
                pl.when(jnp.logical_not(far))(copy.start)

    def far(self, offset):
        return self.tp == (0 if offset == 3 else 3)

    def relay(self):
        if not self.line or self.relayed:
            return
        self.relayed = True
        target = lax.rem(self.tp + 2, self.parts)

        @pl.when(self.inner)
        def _():
            self.vias[3].wait_recv()
            joined = self.part[target].astype(F32) + self.landed[0].astype(F32)
            self.part[target] = joined.astype(BF)
            self.copies[2].start()

        for offset in (1, 3):

            @pl.when(self.tp == (0 if offset == 1 else 3))
            def _(offset=offset):
                self.landed[offset] = jnp.zeros(self.landed.shape[1:], BF)

    def total(self):
        self.relay()
        total = self.part[self.tp].astype(F32)
        for offset in sorted(self.copies):
            wait = self.copies[offset].wait_recv
            if self.line and offset != 2:
                pl.when(self.tp != (0 if offset == 1 else 3))(wait)
            else:
                wait()
            total = total + self.landed[offset].astype(F32)
        return total

    def wait_send(self):
        for copy in self.copies.values():
            copy.wait_send()


def placed(index, segments):
    place = index
    for start, first in segments:
        place = jnp.where(index >= start, index - start + first, place)
    return place


def request_at(position, ends):
    request = jnp.zeros(position.shape, jnp.int32)
    for end in ends[:-1]:
        request = request + jnp.where(position >= end, 1, 0)
    return request


def add_all(buffer):
    total = buffer[0]
    for i in range(1, buffer.shape[0]):
        total = total + buffer[i]
    return total


def row_scale(squares, width):
    return lax.rsqrt(rows_to_columns(add_all(squares)) / width + norm_eps)


def square_sums(values):
    return jnp.sum(values * values, axis=1, keepdims=True)


def add_keys(query, key, value, mask, numer, denom, head, first=0):
    rows = slice(first, first + query.shape[0])
    cols = slice(head * HD, (head + 1) * HD)
    scores = dot_t(query, key) * HD ** (-0.5)
    weights = jnp.where(mask, jnp.exp(scores), 0.0)
    lanes = denom[head, rows, :]
    rest = weights.shape[1] % HD
    if rest:
        empty = jnp.zeros((weights.shape[0], HD - rest), F32)
        lanes = lanes + jnp.concatenate([weights[:, weights.shape[1] - rest :], empty], axis=1)
    for start in range(0, weights.shape[1] - rest, HD):
        lanes = lanes + weights[:, start : start + HD]
    denom[head, rows, :] = lanes
    numer[rows, cols] = numer[rows, cols] + dot(weights.astype(BF), value)


def finish(numer, denom, mix, keep, first):
    parts, size, width = mix.shape
    rows = slice(first, first + parts * size)
    for head in range(width // HD):
        cols = slice(head * HD, (head + 1) * HD)
        total = jnp.sum(denom[head, rows, :], axis=1, keepdims=True)
        mixed = numer[rows, cols] / total
        if keep is not None:
            mixed = mixed * keep[:, cols]
        mix[:, :, cols] = mixed.astype(BF).reshape(parts, size, HD)


def noise_level(step_value):
    fraction = 1.0 - step_value / STEPS
    return flow_shift * fraction / (1.0 + (flow_shift - 1.0) * fraction)


def block_kernel(
    sizes, chunk_units, names, chunk_names, *refs,
):
    ref = types.SimpleNamespace(**dict(zip(names, refs)))
    rest = refs[len(names) :]
    per = []
    for c in range(len(sizes)):
        mine = rest[c * len(chunk_names) : (c + 1) * len(chunk_names)]
        per.append(types.SimpleNamespace(**dict(zip(chunk_names, mine, strict=True))))
    counts, lens, steps, mod, states = ref.counts, ref.lens, ref.steps, ref.mod, ref.states
    gains = ref.gains
    rows, width = states.shape
    cols = ref.self_out.shape[0]
    core, tp, req = lax.axis_index("cfg"), lax.axis_index("tp"), lax.axis_index("req")
    parts, blocks = lax.axis_size("tp"), lax.axis_size("req")
    block_rows = rows * parts
    heads = cols // HD
    requests = counts.shape[0]
    mate = {"cfg": 1 - core}

    def fetch(i, source, target):
        copy = pltpu.make_async_copy(source, target, ref.fetch_sem.at[i])
        copy.start()
        return copy

    fetches = types.SimpleNamespace(
        qkv=fetch(0, ref.qkv, ref.v_qkv),
        text=fetch(1, ref.text, ref.v_text),
        self_out=fetch(2, ref.self_out, ref.v_self_out),
        cross_query=fetch(3, ref.cross_query, ref.v_cross_query),
        cross_out=fetch(4, ref.cross_out, ref.v_cross_out),
        ffn_in=fetch(5, ref.ffn_in, ref.v_ffn_in),
        ffn_out=fetch(6, ref.ffn_out, ref.v_ffn_out),
    )
    greet(others("tp") + others("req") + [mate])

    starts = [sum(sizes[:c]) for c in range(len(sizes))]
    chunks = range(len(sizes))
    spans = [slice(starts[c], starts[c] + sizes[c]) for c in chunks]
    key_starts = [parts * start for start in starts]
    segments = [
        [(t * sizes[c], t * rows + starts[c]) for t in range(parts)] for c in chunks
    ]
    all_segments = [
        (key_starts[c] + start, first) for c in chunks for start, first in segments[c]
    ]
    ends = request_bounds(counts)
    row_first = (req * parts + tp) * rows
    request = [
        request_at(
            row_first + starts[c] + lax.broadcasted_iota(jnp.int32, (sizes[c], 1), 0), ends
        )
        for c in chunks
    ]
    keep = keep_columns(cols)
    done = []

    rows_self = [per[c].rows_self for c in chunks]
    gathers = []
    for c in chunks:
        rows_self[c][tp] = (
            layer_norm(states[spans[c], :]) * (1.0 + mod_rows(mod, request[c], 1))
            + mod_rows(mod, request[c], 0)
        ).astype(BF)
        gathers.append(Gather(rows_self[c], ref.ag_send, ref.ag_recv, c, True))
    numer, denom = ref.numer, ref.denom
    numer[...] = jnp.zeros_like(numer)
    denom[...] = jnp.zeros_like(denom)

    fetches.text.wait()
    text, text_squares, text_keys = ref.v_text, ref.text_squares, ref.text_keys
    text_squares[tp] = columns_to_rows(
        [square_sums(kept(text[r, 0].astype(F32), keep)) for r in range(requests)]
    )
    text_copies = Gather(text_squares, ref.tx_send, ref.tx_recv, 0)

    fetches.qkv.wait()
    qkv, keys, values, query = ref.v_qkv, ref.keys, ref.values, ref.query

    def block_copy(buffer, send, recv, c, offset):
        span = pl.ds(key_starts[c], parts * sizes[c])
        return remote(
            buffer.at[req, span],
            buffer.at[req, span],
            send.at[c, offset],
            recv.at[c, offset],
            {"req": lax.rem(req + offset, blocks)},
        )

    def key_copy(c, offset):
        return block_copy(keys, ref.k_send, ref.k_recv, c, offset)

    def value_copy(c, offset):
        return block_copy(values, ref.v_send, ref.v_recv, c, offset)

    def start_all(make, c):
        def body(offset, carry):
            make(c, offset).start()
            return carry

        lax.fori_loop(1, blocks, body, 0)

    raws, square_copies = [], []
    for c in chunks:
        gathers[c].wait_recv()
        full = rows_self[c][...].reshape(parts * sizes[c], width)
        key_span = slice(key_starts[c], key_starts[c] + parts * sizes[c])
        values[req, key_span, :] = dot(full, qkv[2]).astype(BF)
        start_all(value_copy, c)
        raw_k = kept(dot(full, qkv[1]), keep)
        raw_q = kept(dot(full, qkv[0]), keep)
        squares = per[c].squares_self
        squares[tp] = columns_to_rows([square_sums(raw_q), square_sums(raw_k)])
        square_copies.append(Gather(squares, ref.sq_send, ref.sq_recv, c))
        for later in gathers[c + 1 :]:
            later.relay()
        square_copies[c].wait_recv()
        scale = row_scale(squares, width)
        keys[req, key_span, :] = (raw_k * scale[:, 1:2] * gains[1:2, :]).astype(BF)
        start_all(key_copy, c)
        query[key_span, :] = (raw_q * scale[:, 0:1] * gains[0:1, :]).astype(BF)
    done += gathers + square_copies

    key_places = [
        placed(lax.broadcasted_iota(jnp.int32, (1, parts * sizes[c]), 1), segments[c])
        for c in chunks
    ]
    query_request = request_at(
        req * block_rows
        + placed(lax.broadcasted_iota(jnp.int32, (block_rows, 1), 0), all_segments),
        ends,
    )
    lows = pick(query_request, [jnp.int32(0)] + ends[:-1])
    highs = pick(query_request, ends)

    def attend(slot, c):
        place = slot * block_rows + key_places[c]
        key_span = slice(key_starts[c], key_starts[c] + parts * sizes[c])
        mask = (place >= lows) & (place < highs)
        for head in range(heads):
            span = slice(head * HD, (head + 1) * HD)
            add_keys(
                query[:, span],
                keys[slot, key_span, span],
                values[slot, key_span, span],
                mask,
                numer,
                denom,
                head,
            )

    for c in chunks:
        attend(req, c)
    text_copies.wait_recv()
    done.append(text_copies)
    scale = row_scale(text_squares, width)
    for r in range(requests):
        raw = kept(text[r, 0].astype(F32), keep)
        text_keys[r] = (raw * scale[:, r : r + 1] * gains[3:4, :]).astype(BF)

    for c in chunks:

        def visit(offset, carry, c=c):
            value_copy(c, offset).wait_recv()
            key_copy(c, offset).wait_recv()
            attend(lax.rem(req + blocks - offset, blocks), c)
            return carry

        lax.fori_loop(1, blocks, visit, 0)

    fetches.self_out.wait()
    mixes = [per[c].mix for c in chunks]

    def project(c, weight, part):
        flat = mixes[c][...].reshape(parts * sizes[c], cols)
        part[...] = dot(flat, weight[...]).astype(BF).reshape(part.shape)

    scatters = []
    for c in chunks:
        finish(numer, denom, mixes[c], keep, key_starts[c])
        project(c, ref.v_self_out, per[c].part_self)
        scatters.append(
            Scatter(per[c].part_self, per[c].landed_self, ref.rs_self_send, ref.rs_self_recv, c)
        )

    rows_cross = [per[c].rows_cross for c in chunks]
    hidden, gathers = [], []
    for item in scatters:
        item.relay()
    for c in chunks:
        delta = scatters[c].total()
        hidden_one = states[spans[c], :] + mod_rows(mod, request[c], 2) * delta
        ref.hidden[spans[c], :] = hidden_one
        rows_cross[c][tp] = (layer_norm(hidden_one) * ref.cross_gain[...].reshape(1, width)).astype(BF)
        gathers.append(Gather(rows_cross[c], ref.cg_send, ref.cg_recv, c, True))
        done += [scatters[c], gathers[c]]
    numer[...] = jnp.zeros_like(numer)
    denom[...] = jnp.zeros_like(denom)
    fetches.cross_query.wait()
    fetches.cross_out.wait()
    slots = text.shape[2]
    text_place = lax.broadcasted_iota(jnp.int32, (1, slots), 1)
    scatters = []
    for c in chunks:
        gathers[c].wait_recv()
        count = parts * sizes[c]
        raw_q = kept(dot(rows_cross[c][...].reshape(count, width), ref.v_cross_query[...]), keep)
        squares = per[c].squares_cross
        squares[tp] = columns_to_rows([square_sums(raw_q)])
        copies = Gather(squares, ref.cs_send, ref.cs_recv, c)
        done.append(copies)
        for earlier in scatters:
            earlier.relay()
        for later in gathers[c + 1 :]:
            later.relay()
        copies.wait_recv()
        scale = row_scale(squares, width)
        cross_q = (raw_q * scale[:, 0:1] * gains[2:3, :]).astype(BF)
        query_request = request_at(
            req * block_rows
            + placed(lax.broadcasted_iota(jnp.int32, (count, 1), 0), segments[c]),
            ends,
        )
        for r in range(requests):
            mask = text_place < jnp.where(query_request == r, lens[0, r], 0)
            for head in range(heads):
                span = slice(head * HD, (head + 1) * HD)
                add_keys(
                    cross_q[:, span],
                    text_keys[r, :, span],
                    text[r, 1, :, span],
                    mask,
                    numer,
                    denom,
                    head,
                    key_starts[c],
                )
        finish(numer, denom, mixes[c], keep, key_starts[c])
        project(c, ref.v_cross_out, per[c].part_cross)
        scatters.append(
            Scatter(per[c].part_cross, per[c].landed_cross, ref.rs_cross_send, ref.rs_cross_recv, c)
        )

    rows_ffn = [per[c].rows_ffn for c in chunks]
    gathers = []
    for item in scatters:
        item.relay()
    for c in chunks:
        delta = scatters[c].total()
        hidden_two = ref.hidden[spans[c], :] + delta
        ref.hidden[spans[c], :] = hidden_two
        rows_ffn[c][core, tp] = (
            layer_norm(hidden_two) * (1.0 + mod_rows(mod, request[c], 4))
            + mod_rows(mod, request[c], 3)
        ).astype(BF)
        gathers.append(Gather(rows_ffn[c].at[core], ref.fg_send, ref.fg_recv, c, True))
        done += [scatters[c], gathers[c]]

    def forward(c, offset):
        view = rows_ffn[c].at[core, lax.rem(tp + parts - offset, parts)]
        copy = remote(view, view, ref.fw_send.at[c, offset], ref.fw_recv.at[c, offset], mate)
        copy.start()
        return copy

    forwards = [[forward(c, 0)] for c in chunks]

    def forward_rest(c):
        gathers[c].relay()
        for offset in gathers[c].copies:
            gathers[c].wait_one(offset)
            forwards[c].append(forward(c, offset))

    fetches.ffn_in.wait()
    fetches.ffn_out.wait()
    scatters = []
    forward_rest(0)
    for c in chunks:
        count = parts * sizes[c]
        acc, half, from_core = per[c].acc, per[c].half, per[c].from_core
        for copy in forwards[c]:
            copy.wait_recv()
        full = rows_ffn[c][...].reshape(2 * count, width)
        acc[...] = jnp.zeros_like(acc)

        def step(i, carry, full=full, acc=acc, count=count):
            span = pl.ds(pl.multiple_of(i * chunk_units, 16), chunk_units)
            up = dot_t(full, ref.v_ffn_in[span, :])
            act = jax.nn.gelu(up, approximate=True).astype(BF)
            acc[...] = acc[...] + dot(act, ref.v_ffn_out[span, :]).reshape(2, count, width)
            return carry

        loops = ref.v_ffn_in.shape[0] // chunk_units
        pause = min(2, loops)
        lax.fori_loop(0, pause, step, 0)
        for earlier in scatters:
            earlier.relay()
        for later in gathers[c + 1 :]:
            later.relay()
        lax.fori_loop(pause, loops, step, 0)
        half[...] = acc[1 - core].astype(BF)
        across = remote(half, from_core, ref.core_send.at[c], ref.core_recv.at[c], mate)
        across.start()
        if c + 1 < len(sizes):
            forward_rest(c + 1)
        across.wait_recv()

        total = acc[core] + from_core[...].astype(F32)
        per[c].part_ffn[...] = total.astype(BF).reshape(per[c].part_ffn.shape)
        scatters.append(
            Scatter(per[c].part_ffn, per[c].landed_ffn, ref.rs_ffn_send, ref.rs_ffn_recv, c)
        )
        done += forwards[c] + [across, scatters[c]]

    speed = ref.speed
    for item in scatters:
        item.relay()
    for c in chunks:
        delta = scatters[c].total()
        last = ref.hidden[spans[c], :] + mod_rows(mod, request[c], 5) * delta
        ref.final[spans[c], :] = layer_norm(last).astype(BF)
    speed[0] = dot_t(ref.head[...], ref.final[...])
    swap = remote(speed.at[0], speed.at[1], ref.swap_send, ref.swap_recv, mate)
    swap.start()
    swap.wait_recv()
    done.append(swap)
    own, other = speed[0], speed[1]
    request = request_at(row_first + lax.broadcasted_iota(jnp.int32, (1, rows), 1), ends)
    cond = jnp.where(core == 0, own, other)
    plain = jnp.where(core == 0, other, own)
    guided = plain + guide_scale * (cond - plain)
    lane = lax.broadcasted_iota(jnp.int32, (8, HD), 1)
    line = lax.broadcasted_iota(jnp.int32, (8, HD), 0)
    pack = jnp.zeros((8, HD), F32)
    per_row = [
        jnp.sum(cond * cond, axis=0, keepdims=True),
        jnp.sum(guided * guided, axis=0, keepdims=True),
        jnp.max(jnp.abs(guided), axis=0, keepdims=True),
    ]
    for r in range(requests):
        for i, column in enumerate(per_row):
            chosen = jnp.where(request == r, column, 0.0)
            if i < 2:
                value = jnp.sum(chosen, axis=1, keepdims=True)
            else:
                value = jnp.max(chosen, axis=1, keepdims=True)
            pack = jnp.where((lane == r) & (line == i), value, pack)

    def combine(buffer):
        total, top = buffer[0], buffer[0]
        for i in range(1, buffer.shape[0]):
            total = total + buffer[i]
            top = jnp.maximum(top, buffer[i])
        return jnp.where(line == 2, top, total)

    stats_tp, stats_req = ref.stats_tp, ref.stats_req
    stats_tp[tp] = pack
    stat_copies = [Gather(stats_tp, ref.st_send, ref.st_recv, 0)]
    stat_copies[0].wait_recv()
    stats_req[req] = combine(stats_tp)
    for offset in range(1, blocks):
        copy = remote(
            stats_req.at[req],
            stats_req.at[req],
            ref.sr_send.at[offset],
            ref.sr_recv.at[offset],
            {"req": peer_at("req", offset)},
        )
        copy.start()
        stat_copies.append(copy)
    for copy in stat_copies[1:]:
        copy.wait_recv()
    stats = combine(stats_req)
    lanes = lane[:1]
    count = jnp.ones((1, HD), F32)
    step_value = jnp.zeros((1, HD), F32)
    for r in range(requests):
        count = jnp.where(lanes == r, (counts[r] * guided.shape[0]).astype(F32), count)
        step_value = jnp.where(lanes == r, steps[r].astype(F32), step_value)
    cond_rms = jnp.sqrt(stats[0:1] / count + stat_eps)
    guided_rms = jnp.sqrt(stats[1:2] / count + stat_eps)
    factor = rescale_mix * cond_rms / guided_rms + (1.0 - rescale_mix)
    delta_t = noise_level(step_value + 1.0) - noise_level(step_value)
    ref.peak[...] = factor * stats[2:3]
    row_factor = pick(request, [factor[:, r : r + 1] for r in range(requests)])
    row_step = pick(request, [delta_t[:, r : r + 1] for r in range(requests)])
    velocity = row_factor * guided
    moved = ref.latent[...] + row_step * velocity
    new_latent, velocity_out = ref.new_latent, ref.velocity
    own_cols = velocity_out.shape[0]
    velocity_out[...] = jnp.where(core == 0, velocity[:own_cols], velocity[own_cols:])
    new_latent[...] = jnp.where(core == 0, moved[:own_cols], moved[own_cols:])
    for copy in done + stat_copies:
        copy.wait_send()

    def drain(offset, carry):
        for c in chunks:
            key_copy(c, offset).wait_send()
            value_copy(c, offset).wait_send()
        return carry

    lax.fori_loop(1, blocks, drain, 0)


def shards(
    latent,
    states,
    token_counts,
    text_lens,
    steps_index,
    modulation,
    self_qkv,
    self_out,
    qk_gains,
    cross_query,
    cross_out,
    cross_gain,
    text_kv,
    ffn_in_weight,
    ffn_out_weight,
    head_weight,
):
    rows = latent.shape[0]
    width = head_weight.shape[0]
    cols = self_out.shape[0]
    heads = cols // HD
    parts, blocks = lax.axis_size("tp"), lax.axis_size("req")
    block_rows = rows * parts
    requests, slots = text_kv.shape[1], text_kv.shape[3]
    units = ffn_in_weight.shape[0]
    chunk_units = units // 5 if units % 80 == 0 else units
    first = -(-rows // 32) * 16
    sizes = (first, rows - first)
    V, S, H = pltpu.VMEM, pltpu.SMEM, pl.ANY
    operands = dict(
        counts=(S, token_counts),
        lens=(S, text_lens),
        steps=(S, steps_index),
        mod=(V, modulation),
        states=(V, states[0]),
        gains=(V, qk_gains),
        cross_gain=(V, cross_gain),
        head=(V, jnp.transpose(head_weight)),
        latent=(V, jnp.transpose(latent)),
        qkv=(H, jnp.transpose(self_qkv, (1, 0, 2))),
        text=(H, text_kv[0]),
        self_out=(H, self_out),
        cross_query=(H, cross_query),
        cross_out=(H, cross_out),
        ffn_in=(H, ffn_in_weight),
        ffn_out=(H, ffn_out_weight),
    )
    small = jax.ShapeDtypeStruct((latent.shape[1] // lax.axis_size("cfg"), rows), F32)
    results = dict(new_latent=small, velocity=small, peak=jax.ShapeDtypeStruct((1, HD), F32))

    def sem(*shape):
        return pltpu.SemaphoreType.DMA(shape) if shape else pltpu.SemaphoreType.DMA

    two = len(sizes)
    by_tp, by_req = sem(two, parts), sem(two, blocks)
    scratch = dict(
        v_qkv=V((3, width, cols), BF),
        v_text=V(text_kv.shape[1:], BF),
        v_self_out=V(self_out.shape, BF),
        v_cross_query=V(cross_query.shape, BF),
        v_cross_out=V(cross_out.shape, BF),
        v_ffn_in=V(ffn_in_weight.shape, BF),
        v_ffn_out=V(ffn_out_weight.shape, BF),
        fetch_sem=sem(7),
        keys=V((blocks, block_rows, cols), BF),
        values=V((blocks, block_rows, cols), BF),
        query=V((block_rows, cols), BF),
        numer=V((block_rows, cols), F32),
        denom=V((heads, block_rows, HD), F32),
        text_squares=V((parts, 8, slots), F32),
        text_keys=V((requests, slots, cols), BF),
        hidden=V((rows, width), F32),
        speed=V((2, latent.shape[1], rows), F32),
        final=V((rows, width), BF),
        stats_tp=V((parts, 8, HD), F32),
        stats_req=V((blocks, 8, HD), F32),
        ag_send=by_tp, ag_recv=by_tp,
        sq_send=by_tp, sq_recv=by_tp,
        tx_send=by_tp, tx_recv=by_tp,
        k_send=by_req, k_recv=by_req,
        v_send=by_req, v_recv=by_req,
        rs_self_send=by_tp, rs_self_recv=by_tp,
        cg_send=by_tp, cg_recv=by_tp,
        cs_send=by_tp, cs_recv=by_tp,
        rs_cross_send=by_tp, rs_cross_recv=by_tp,
        fg_send=by_tp, fg_recv=by_tp,
        fw_send=by_tp, fw_recv=by_tp,
        core_send=sem(two), core_recv=sem(two),
        rs_ffn_send=by_tp, rs_ffn_recv=by_tp,
        swap_send=sem(), swap_recv=sem(),
        st_send=by_tp, st_recv=by_tp,
        sr_send=sem(blocks), sr_recv=sem(blocks),
    )

    def chunk_scratch(size):
        count = parts * size
        wide = V((parts, size, width), BF)
        return dict(
            rows_self=wide, rows_cross=wide, rows_ffn=V((2, parts, size, width), BF),
            part_self=wide, landed_self=wide,
            part_cross=wide, landed_cross=wide,
            part_ffn=wide, landed_ffn=wide,
            squares_self=V((parts, 8, count), F32),
            squares_cross=V((parts, 8, count), F32),
            mix=V((parts, size, cols), BF),
            acc=V((2, count, width), F32),
            half=V((count, width), BF),
            from_core=V((count, width), BF),
        )

    chunk_dicts = [chunk_scratch(size) for size in sizes]
    names = tuple(operands) + tuple(results) + tuple(scratch)
    shapes = list(scratch.values()) + [v for d in chunk_dicts for v in d.values()]
    new_latent, velocity, peak = pl.pallas_call(
        functools.partial(block_kernel, sizes, chunk_units, names, tuple(chunk_dicts[0])),
        out_shape=tuple(results.values()),
        in_specs=[pl.BlockSpec(memory_space=space) for space, _ in operands.values()],
        out_specs=tuple(pl.BlockSpec(memory_space=V) for _ in results),
        scratch_shapes=shapes,
        compiler_params=pltpu.CompilerParams(
            collective_id=0, has_side_effects=True, vmem_limit_bytes=VMEM_LIMIT
        ),
        cost_estimate=pl.CostEstimate(
            flops=16 * block_rows * width * units, bytes_accessed=20 << 20, transcendentals=0
        ),
    )(*[value for _, value in operands.values()])
    return jnp.transpose(new_latent), jnp.transpose(velocity), peak[0, :requests]


def solution(mesh):
    in_specs = (
        P(("req", "tp"), None),
        P("cfg", ("req", "tp"), None),
        P(),
        P("cfg", None),
        P(),
        P(),
        P(None, None, "tp"),
        P("tp", None),
        P(None, "tp"),
        P(None, "tp"),
        P("tp", None),
        P(),
        P("cfg", None, None, None, "tp"),
        P(("cfg", "tp"), None),
        P(("cfg", "tp"), None),
        P(),
    )
    out_specs = (P(("req", "tp"), "cfg"), P(("req", "tp"), "cfg"), P())
    return jax.shard_map(shards, mesh=mesh, in_specs=in_specs, out_specs=out_specs, check_vma=False)
```
